128 devices in a mesh: lon: 16 (over z, y_lo, core), lat: 8 (over y_hi, x).
Axes of the slice: x: 4, y: 4 (y_hi: 2, y_lo: 2; y = y_hi * 2 + y_lo), z: 4, core: 2. Of those that a mesh axis runs over, the one named last changes fastest.
Arguments:
- tokens: bfloat16 [2, 192, 576, 512], P(None, 'lat', 'lon'), may hold values from -16 to 16
- gain: float32 [512], replicated, may hold values from 0.1 to 1.9
- qkv_weight: bfloat16 [512, 1536], replicated, may hold values from -8 to 8
- out_weight: bfloat16 [512, 512], replicated, may hold values from -0.25 to 0.25
- cotangent: bfloat16 [2, 192, 576, 512], P(None, 'lat', 'lon'), may hold values from -6 to 6
Outputs:
- output: bfloat16 [2, 192, 576, 512], P(None, 'lat', 'lon')
- d_tokens: bfloat16 [2, 192, 576, 512], P(None, 'lat', 'lon')
- d_qkv_weight: float32 [512, 1536], P(('lon', 'lat'))
- d_out_weight: float32 [512, 512], P(('lon', 'lat'))
The draws below stay inside these ranges and needn't reach their ends.
All inputs are finite; a program needn't handle non-finite values.
Results may differ from the reference program's by a relative error of at most 0.015.
The reference program's roundings to bfloat16 on the way (of `hidden`, `projected`, `weights_bf`, `attended`, `d_attended`, `d_value`, `d_scores` and `d_projected`) count: a program that leaves them out, or rounds other values in their place, can miss the bound.
Values may be sent and summed in bfloat16 or wider, within the bound.
A program may use at most 128 MiB of HBM per device.

```python
import jax
import jax.numpy as jnp
from jax import lax

D = 512
HEAD = 32
LEV = 2
WIN_LAT = 6
WIN_LON = 12
NH = 192
NW = 576
TOKENS = 221184


def draw_tokens(key, part):
    key = jax.random.fold_in(key, 11)
    base_key = jax.random.fold_in(key, 0)
    base = jax.random.normal(base_key, (LEV, NH, NW, D), jnp.float32)
    return jnp.clip(base, -6.0, 6.0).astype(jnp.bfloat16)


def draw_qkv_weight(key, part):
    key = jax.random.fold_in(key, 23)
    first_key, second_key, third_key = jax.random.split(key, 3)
    spread = D ** (-0.5)
    query_part = jax.random.normal(first_key, (D, D), jnp.float32) * spread
    value_part = jax.random.normal(third_key, (D, D), jnp.float32) * spread
    key_part = jax.random.normal(second_key, (D, D), jnp.float32) * spread
    return jnp.clip(jnp.concatenate([query_part, key_part, value_part], 1), -6.0 * spread, 6.0 * spread).astype(jnp.bfloat16)


def level_of(stream_key, shape, shards, least, largest):
    def one(axis_at, shards_of):
        heights = jax.random.uniform(jax.random.fold_in(jax.random.fold_in(stream_key, 6), axis_at), (shards_of,), jnp.float32, least / len(shards), largest / len(shards))
        return jnp.repeat(jnp.exp(heights), shape[axis_at] // shards_of).reshape((-1,) + (1,) * (len(shape) - axis_at - 1))

    level = one(*shards[0])
    for cut in shards[1:]:
        level = level * one(*cut)
    return level


def centred(stream_key, shape, width, limit, pieces=(), kind=jnp.bfloat16):
    entries = jax.random.normal(stream_key, shape, jnp.float32) * width
    if len(pieces) > 0:
        entries = level_of(stream_key, shape, pieces, -0.22, 0.18) * entries
    return jnp.clip(entries, min=-limit, max=limit).astype(kind)


def setup_inputs(seed: int = 0) -> dict:
    seeds = jax.random.split(jax.random.key(seed), 6)
    return {
        "tokens": draw_tokens(jax.random.fold_in(seeds[5], 71), 0),
        "gain": jnp.clip(1.0 + 0.18 * jax.random.normal(seeds[1], (D,), jnp.float32), 0.1, 1.9),
        "qkv_weight": draw_qkv_weight(jax.random.fold_in(seeds[5], 71), 0),
        "out_weight": centred(seeds[3], (D, D), D ** -0.5, 0.25),
        "cotangent": centred(seeds[4], (LEV, NH, NW, D), 1.0, 6.0, ((1, 8), (2, 16))),
    }


epsilon = 1e-05

def normalize(values_in):
    values = values_in.astype(jnp.float32)
    centre = values - lax.optimization_barrier(jnp.mean(values, -1, keepdims=True))
    inverse = lax.rsqrt(lax.optimization_barrier(jnp.mean(centre * centre, -1, keepdims=True)) + epsilon)
    return (centre * inverse, inverse)

def reference(tokens, gain, qkv_weight, out_weight, cotangent):
    head_count = D // HEAD
    half_lat = WIN_LAT // 2
    half_lon = WIN_LON // 2
    wide_count = NW // WIN_LON
    window_len = LEV * WIN_LAT * WIN_LON
    score_scale = HEAD ** (-0.5)
    row_count = NH // WIN_LAT
    rolled = jnp.roll(tokens, (-half_lat, -half_lon), axis=(1, 2))
    grad_rolled = jnp.roll(cotangent, (-half_lat, -half_lon), axis=(1, 2))
    slabs = rolled.reshape(LEV, row_count, WIN_LAT, NW, D).transpose(1, 0, 2, 3, 4)
    grad_slabs = grad_rolled.reshape(LEV, row_count, WIN_LAT, NW, D).transpose(1, 0, 2, 3, 4)
    row_ids = jnp.arange(row_count, dtype=jnp.int32)[:, None] * WIN_LAT + jnp.arange(WIN_LAT, dtype=jnp.int32)[None, :]
    sides = row_ids >= NH - half_lat

    def windows(source):
        return source.reshape(LEV, WIN_LAT, wide_count, WIN_LON, -1).transpose(2, 0, 1, 3, 4).reshape(wide_count, window_len, -1)

    def unwindow(source):
        return source.reshape(wide_count, LEV, WIN_LAT, WIN_LON, -1).transpose(1, 2, 0, 3, 4).reshape(LEV, WIN_LAT, NW, -1)

    def slab_step(totals, inputs):
        slab_x, grad_slab, side_flag = inputs
        normed, inverse = normalize(slab_x)
        hidden = (normed * gain).astype(jnp.bfloat16)
        hidden_win = windows(hidden).reshape(-1, D)
        grad_win = windows(grad_slab).reshape(-1, D)
        projected = jnp.dot(hidden_win, qkv_weight, preferred_element_type=jnp.float32).astype(jnp.bfloat16)
        projected = projected.reshape(wide_count, window_len, 3, head_count, HEAD).astype(jnp.float32)
        query = projected[:, :, 0]
        key_part = projected[:, :, 1]
        value_part = projected[:, :, 2]
        d_attended = jnp.dot(grad_win, out_weight.T, preferred_element_type=jnp.float32).astype(jnp.bfloat16)
        d_attended = d_attended.reshape(wide_count, window_len, head_count, HEAD).astype(jnp.float32)
        flags = jnp.broadcast_to(side_flag[None, :, None], (LEV, WIN_LAT, WIN_LON)).reshape(window_len)
        allowed = flags[:, None] == flags[None, :]
        scores = jnp.einsum('wqhe,wkhe->whqk', query, key_part) * score_scale
        scores = jnp.where(allowed, scores, -1e+30)
        peak = lax.optimization_barrier(jnp.max(scores, -1, keepdims=True))
        expo = jnp.exp(scores - peak)
        weights = expo / lax.optimization_barrier(jnp.sum(expo, -1, keepdims=True))
        weights_bf = weights.astype(jnp.bfloat16).astype(jnp.float32)
        attended = jnp.einsum('whqk,wkhe->wqhe', weights_bf, value_part).astype(jnp.bfloat16)
        attended_flat = attended.reshape(-1, D)
        proj = jnp.dot(attended_flat, out_weight, preferred_element_type=jnp.float32)
        output_slab = (slab_x.astype(jnp.float32) + unwindow(proj.reshape(wide_count, window_len, D))).astype(jnp.bfloat16)
        d_weights = jnp.einsum('wqhe,wkhe->whqk', d_attended, value_part)
        d_value = jnp.einsum('whqk,wqhe->wkhe', weights_bf, d_attended).astype(jnp.bfloat16)
        d_scores = weights * (d_weights - lax.optimization_barrier(jnp.sum(weights * d_weights, -1, keepdims=True))) * score_scale
        d_scores = d_scores.astype(jnp.bfloat16).astype(jnp.float32)
        d_query = jnp.einsum('whqk,wkhe->wqhe', d_scores, key_part).astype(jnp.bfloat16)
        d_key = jnp.einsum('whqk,wqhe->wkhe', d_scores, query).astype(jnp.bfloat16)
        d_projected = jnp.stack([d_query, d_key, d_value], 2).reshape(-1, 3 * D)
        d_hidden = jnp.dot(d_projected, qkv_weight.T, preferred_element_type=jnp.float32)
        d_hidden = unwindow(d_hidden.reshape(wide_count, window_len, D))
        unit = d_hidden * gain
        d_slab = grad_slab.astype(jnp.float32) + inverse * (unit - lax.optimization_barrier(jnp.mean(unit, -1, keepdims=True)) - normed * lax.optimization_barrier(jnp.mean(unit * normed, -1, keepdims=True)))
        qkv_term = jnp.dot(hidden_win.T, d_projected, preferred_element_type=jnp.float32)
        out_term = jnp.dot(attended_flat.T, grad_win, preferred_element_type=jnp.float32)
        return ((totals[0] + qkv_term, totals[1] + out_term), (output_slab, d_slab.astype(jnp.bfloat16)))
    start_totals = (jnp.zeros((D, 3 * D), jnp.float32), jnp.zeros((D, D), jnp.float32))
    totals, (out_slabs, d_slabs) = lax.scan(slab_step, start_totals, (slabs, grad_slabs, sides))
    output = out_slabs.transpose(1, 0, 2, 3, 4).reshape(LEV, NH, NW, D)
    d_tokens = d_slabs.transpose(1, 0, 2, 3, 4).reshape(LEV, NH, NW, D)
    output = jnp.roll(output, (half_lat, half_lon), axis=(1, 2))
    d_tokens = jnp.roll(d_tokens, (half_lat, half_lon), axis=(1, 2))
    grad_scale = TOKENS ** (-0.5)
    return (output, d_tokens, totals[0] * grad_scale, totals[1] * grad_scale)
```

```python
import functools
import math

import jax
import jax.numpy as jnp
import numpy as np
from jax import lax
from jax.experimental import pallas as pl
from jax.experimental.pallas import tpu as pltpu
from jax.sharding import PartitionSpec as P

F32, BF16 = jnp.float32, jnp.bfloat16
MESH = pl.DeviceIdType.MESH
D = 512
HEAD = 32
CELLS = 1728
WIN = 144
EPS = 1e-5
NN = (((1,), (0,)), ((), ()))
NT = (((1,), (1,)), ((), ()))
TN = (((0,), (0,)), ((), ()))
SCALE = HEAD**-0.5
SCALE_LOG2E = SCALE * math.log2(math.e)


def dot(a, b, dims=NN):
    return lax.dot_general(a, b, dims, preferred_element_type=F32)


def tables():
    order = np.zeros((192, 224), np.float32)
    place = np.zeros((192, 224), np.float32)
    squeeze = np.zeros((32, 192), np.float32)
    late = np.zeros((32, 48), np.float32)
    fill = np.zeros((144, 176), np.float32)
    for c in range(8):
        for rho in range(24):
            cell = (rho // 6) * 48 + c * 6 + rho % 6
            if rho < 21:
                order[cell, c * 24 + 3 + rho] = 1
                place[c * 24 + 3 + rho, cell] = 1
            else:
                order[cell, 192 + c * 4 + rho - 21] = 1
                place[c * 24 + rho - 21, 192 + c * 4 + rho - 21] = 1
                late[c * 4 + rho - 21, c * 6 + rho % 6] = 1
                squeeze[c * 4 + rho - 21, c * 24 + rho - 21] = 1
    for c in range(6):
        for row in range(24):
            fill[c * 24 + row, c * 24 + row if row >= 3 else 144 + 8 + c * 4 + row] = 1
    heads = np.zeros((128, 256), np.float32)
    for h in range(8):
        heads[16 * h : 16 * h + 16, 32 * h : 32 * h + 32] = 1
    bf = [jnp.asarray(t, BF16) for t in (order, place, squeeze, late, fill, heads)]
    return bf + [jnp.asarray(heads, F32)]


def groups(strip):
    c = 12 * strip
    return [[(0, c, 8)], [(0, c + 8, 4), (1, c, 4)], [(1, c + 4, 8)]]


def slot(strip, i):
    if strip < 2:
        return strip * 3 + i if i < 3 else 6 + strip
    return 8 + i


def attend(w, j, proj, datt, bias, hm, hmf, att, dproj, pt, st):
    rows = pl.ds(pl.multiple_of(w * WIN, 16), WIN)
    lo = 256 * j
    q = proj[rows, lo : lo + 256]
    k = proj[rows, 512 + lo : 768 + lo]
    v = proj[rows, 1024 + lo : 1280 + lo]
    da = datt[rows, lo : lo + 256]
    vt, kt = v.T, k.T

    def diagonal(x, c):
        if c == 4:
            return jnp.concatenate([x[128:144]] * 8, 0) * hm[...]
        one = [
            x[:128] * jnp.concatenate([hm[16 * h : 16 * h + 16, :]] * 8, 0)
            for h in (2 * c, 2 * c + 1)
        ]
        return jnp.concatenate(one, 0)

    qd = [diagonal(q, c) for c in range(5)]
    dd = [diagonal(da, c) for c in range(5)]
    am, qm = [], []
    for c in range(5):
        n = 256 if c < 4 else 128
        at = slice(256 * c, 256 * c + n)
        s = dot(k, qd[c], NT) + (bias[:, :256] if c < 4 else bias[:, 256:384])
        dw = dot(v, dd[c], NT)
        e = jnp.exp2((s - jnp.max(s, 0, keepdims=True)) * SCALE_LOG2E)
        p = e * (1.0 / jnp.sum(e, 0, keepdims=True))
        ds = p * (dw - jnp.sum(p * dw, 0, keepdims=True)) * SCALE
        p, ds = p.astype(BF16), ds.astype(BF16)
        pt[:, at] = p
        st[:, at] = ds
        if c < 4:
            a = dot(vt[64 * c : 64 * c + 64], p)
            am += [a[:32, :128], a[32:, 128:]]
            a = dot(kt[64 * c : 64 * c + 64], ds)
            qm += [a[:32, :128], a[32:, 128:]]
        else:
            a_end = (dot(p, v, TN) * hmf[...]).reshape(8, 16, 256).sum(0)
            q_end = (dot(ds, k, TN) * hmf[...]).reshape(8, 16, 256).sum(0)
    dv = dot(pt[...], jnp.concatenate(dd, 0))
    dk = dot(st[...], jnp.concatenate(qd, 0))
    join = lambda main, end: jnp.concatenate([jnp.concatenate(main, 0).T, end], 0).astype(BF16)
    att[rows, lo : lo + 256] = join(am, a_end)
    dproj[rows, lo : lo + 256] = join(qm, q_end)
    dproj[rows, 512 + lo : 768 + lo] = dk.astype(BF16)
    dproj[rows, 1024 + lo : 1280 + lo] = dv.astype(BF16)


def kernel(
    tok, cot, gain, wqkv, wo, order, place, squeeze, late, fill, hm, hmf,
    out, dtok, dqkv, dwo,
    own, edge, halo, corner, lsend, region, lout, lonin, latin, cornerin,
    tw, cw, hid, hidt, attt, inv, mean, proj, datt, att, dproj, bias, pt, st,
    gw, r0, s1a, r1a, s1b, r1b, s2a, r2a, s2b, r2b, s3, r3,
    local, send, recv,
):
    lon, lat = lax.axis_index("lon"), lax.axis_index("lat")
    lons, lats = lax.axis_size("lon"), lax.axis_size("lat")
    z, yl, core = lon // 4, (lon // 2) % 2, lon % 2
    yh, x = lat // 4, lat % 4
    west, east = (lon + lons - 1) % lons, (lon + 1) % lons
    south, north = (lat + lats - 1) % lats, (lat + 1) % lats
    dev = lambda a, b: {"lon": a, "lat": b}
    flip = lambda bit: 1 - bit
    twin = dev(z * 4 + yl * 2 + flip(core), lat)
    zs = [(z + d) % 4 for d in (1, 2, 3)]
    xs = [(x + d) % 4 for d in (1, 2, 3)]
    ys = [(flip(yl), yh), (yl, flip(yh)), (flip(yl), flip(yh))]
    zdev = [dev(a * 4 + yl * 2 + core, lat) for a in zs]
    ydev = [dev(z * 4 + a * 2 + core, b * 4 + x) for a, b in ys]
    xdev = [dev(lon, yh * 4 + a) for a in xs]

    loads = []
    for a, ref in enumerate((tok, cot)):
        loads.append(
            pltpu.make_async_copy(ref.at[:, 144:864], own.at[a, :, 0:720], local.at[2 * a])
        )
        loads.append(pltpu.make_async_copy(ref.at[:, 0:144], edge.at[a], local.at[2 * a + 1]))
    for copy in loads:
        copy.start()
    barrier = pltpu.get_barrier_semaphore()
    halo_devs = [dev(west, lat), dev(lon, south), dev(west, south)]
    halo_devs += [dev(east, lat), dev(lon, north), dev(east, north)]
    for target in halo_devs + [twin] + zdev + ydev + xdev:
        pl.semaphore_signal(barrier, inc=1, device_id=target, device_id_type=MESH)
    pl.semaphore_wait(barrier, 16)

    used = [0]

    def remote(src, dst, target):
        n = used[0]
        used[0] += 1
        return pltpu.make_async_remote_copy(
            src_ref=src,
            dst_ref=dst,
            send_sem=send.at[n],
            recv_sem=recv.at[n],
            device_id=target,
            device_id_type=MESH,
        )

    sends = []
    first = []
    for a, ref in enumerate((tok, cot)):
        first.append(remote(ref.at[:, 0:144], own.at[a, :, 720:864], dev(west, lat)))
        first[-1].start()
    latin[:, :, 128:144, :] = jnp.zeros((2, 2, 16, D), BF16)
    for copy in loads:
        copy.wait()

    def pairs_of(a, level, column, count):
        got = []
        here = min(count, max(0, 30 - column))
        if here:
            got.append(own[a, level, column * 24 : (column + here) * 24, :])
        if count - here:
            c = column + here - 30
            got.append(edge[a, level, c * 24 : (c + count - here) * 24, :])
        return got

    for a in range(2):
        for level in range(2):
            for column, count in ((0, 8), (8, 8), (16, 8), (24, 8), (32, 4)):
                cells = jnp.concatenate(pairs_of(a, level, column, count), 0)
                small = dot(squeeze[: count * 4, : count * 24], cells).astype(BF16)
                lsend[a, level, column * 4 : (column + count) * 4, :] = small
        first.append(remote(lsend.at[a, :, 0:128], halo.at[a, :, 0:128], dev(lon, south)))
        first.append(remote(lsend.at[a, :, 112:144], corner.at[a], dev(west, south)))
        first[-2].start()
        first[-1].start()

    def gather(a, strip, g, which):
        runs = groups(strip)[g]
        cells = [own[a, lev, c * 24 : (c + n) * 24, :] for lev, c, n in runs]
        lo, hi = which
        width = 192
        if hi == 4:
            cells += [halo[a, lev, c * 4 : (c + n) * 4, :] for lev, c, n in runs]
            width = 224
        got = dot(order[48 * lo : 48 * hi, :width], jnp.concatenate(cells, 0)).astype(BF16)
        for i in range(lo, hi):
            at = slot(strip, i) * WIN + g * 48
            (tw, cw)[a][at : at + 48, :] = got[(i - lo) * 48 : (i - lo) * 48 + 48]

    @pl.loop(0, 2)
    def _(part):
        @pl.when(part == 0)
        def _():
            for a in range(2):
                for strip in range(2):
                    for g in range(3):
                        gather(a, strip, g, (0, 3))

        @pl.when(part == 1)
        def _():
            for copy in first:
                copy.wait()
            late_row = lax.broadcasted_iota(jnp.int32, (32, D), 0) >= 8
            for a in range(2):
                for level in range(2):
                    halo[a, level, 112:144, :] = jnp.where(
                        late_row, corner[a, level], halo[a, level, 112:144, :]
                    )
                for g in range(3):
                    for strip in range(2):
                        gather(a, strip, g, (3, 4))
                    gather(a, 2, g, (0, 4))

        @pl.loop(0, 3)
        def _(t):
            rows = pl.ds(pl.multiple_of(part * 864 + t * 288, 16), 288)
            cells = tw[rows, :].astype(F32)
            mu = jnp.mean(cells, -1, keepdims=True)
            cells = cells - mu
            iv = lax.rsqrt(jnp.mean(cells * cells, -1, keepdims=True) + EPS)
            h = (cells * iv * gain[...]).astype(BF16)
            hid[rows, :] = h
            mean[rows, :] = mu
            inv[rows, :] = iv
            for n in range(3):
                at = slice(512 * n, 512 * n + 512)
                proj[rows, at] = dot(h, wqkv[:, at]).astype(BF16)
            datt[rows, :] = dot(cw[rows, :], wo[...], NT).astype(BF16)

        @pl.loop(part * 6, part * 6 + 6)
        def _(w):
            key_side = (lax.broadcasted_iota(jnp.int32, (WIN, 1), 0) % 6) >= 3
            lane = lax.broadcasted_iota(jnp.int32, (1, 384), 1)
            query = jnp.where(lane < 256, lane % 128, 128 + lane % 16)
            query_side = (query % 6) >= 3
            last = jnp.logical_or(jnp.logical_or(w == 6, w == 7), w == 11)
            apart = jnp.logical_and(last, lat == lats - 1)
            bias[...] = jnp.where(jnp.logical_and(apart, key_side != query_side), -1e30, 0.0)
            for j in range(2):
                attend(w, j, proj, datt, bias, hm, hmf, att, dproj, pt, st)

    grad_scale = 1.0 / math.sqrt(CELLS * 128)
    hidt[...] = hid[...].T
    attt[...] = att[...].T
    cores = []
    for half in range(2):
        for n in range(4 * half, 4 * half + 4):
            lo = 256 * n
            if n < 6:
                grad = dot(hidt[...], dproj[:, lo : lo + 256])
            else:
                grad = dot(attt[...], cw[:, lo - 1536 : lo - 1280])
            gw[:, :, :, lo : lo + 256] = (grad * grad_scale).reshape(8, 2, 32, 256)
        cols = slice(1024 * half, 1024 * half + 1024)
        cores.append(remote(gw.at[:, flip(core), :, cols], r0.at[:, :, cols], twin))
        cores[-1].start()

    res = (hid, datt)

    def outputs(w):
        rows = pl.ds(pl.multiple_of(w * WIN, 16), WIN)
        cells = tw[rows, :].astype(F32)
        res[0][rows, :] = (cells + dot(att[rows, :], wo[...])).astype(BF16)
        u = dot(dproj[rows, :], wqkv[...], NT) * gain[...]
        iv = inv[rows, :]
        normed = (cells - mean[rows, :]) * iv
        d = u - jnp.mean(u, -1, keepdims=True) - normed * jnp.mean(u * normed, -1, keepdims=True)
        res[1][rows, :] = (cw[rows, :].astype(F32) + iv * d).astype(BF16)

    def windows_of(a, strip, g):
        at = [slot(strip, i) * WIN + g * 48 for i in range(4)]
        return [res[a][n : n + 48, :] for n in at]

    pl.loop(6, 12)(outputs)

    for a in range(2):
        for strip in range(3):
            for g, runs in enumerate(groups(strip)):
                cells = windows_of(a, strip, g)
                small = dot(late[...], cells[3]).astype(BF16)
                at = 0
                for lev, c, n in runs:
                    lout[a, lev, c * 4 : (c + n) * 4, :] = small[at * 4 : (at + n) * 4]
                    at += n
                if strip == 2:
                    whole = dot(place[:, :192], jnp.concatenate(cells, 0)).astype(BF16)
                    at = 0
                    for lev, c, n in runs:
                        region[a, lev, c * 24 : (c + n) * 24, :] = whole[at * 24 : (at + n) * 24]
                        at += n
        sends.append(remote(region.at[a, :, 720:864], lonin.at[a], dev(east, lat)))
        sends.append(remote(lout.at[a, :, 0:128], latin.at[a, :, 0:128], dev(lon, north)))
        sends.append(remote(lout.at[a, :, 112:144], cornerin.at[a], dev(east, north)))
        for copy in sends[-3:]:
            copy.start()

    cores[0].wait()
    stage1 = []
    for k in range(8):
        total = gw[k, core, :, 0:1024] + r0[k, :, 0:1024]
        gw[k, core, :, 0:1024] = total
        s1a[k // 2, k % 2] = total.astype(BF16)
    for d in range(3):
        stage1.append(remote(s1a.at[zs[d]], r1a.at[d], zdev[d]))
        stage1[-1].start()
    cores[1].wait()
    for k in range(8):
        total = gw[k, core, :, 1024:2048] + r0[k, :, 1024:2048]
        gw[k, core, :, 1024:2048] = total
        low = total.astype(BF16)
        for h in range(2):
            s1b[k % 2, h, k // 2] = low[16 * h : 16 * h + 16]
    for d in range(3):
        stage1.append(remote(s1b.at[ys[d][0], ys[d][1]], r1b.at[d], ydev[d]))
        stage1[-1].start()

    pl.loop(0, 6)(outputs)

    stage2 = []
    for copy in stage1[:3]:
        copy.wait()
    for k in range(2):
        total = gw[z * 2 + k, core, :, 0:1024]
        for d in range(3):
            total = total + r1a[d, k].astype(F32)
        for h in range(2):
            s2a[k, h] = total[16 * h : 16 * h + 16]
    for d in range(3):
        stage2.append(remote(s2a.at[ys[d][0], ys[d][1]], r2a.at[d], ydev[d]))
        stage2[-1].start()
    for copy in stage1[3:]:
        copy.wait()
    for k in range(4):
        mine = pl.ds(pl.multiple_of(yh * 16, 16), 16)
        total = gw[k * 2 + yl, core, mine, 1024:2048]
        for d in range(3):
            total = total + r1b[d, k].astype(F32)
        s2b[k] = total
    for d in range(3):
        stage2.append(remote(s2b.at[zs[d]], r2b.at[d], zdev[d]))
        stage2[-1].start()

    for copy in sends:
        copy.wait()
    for a in range(2):
        for level in range(2):
            edge_in = jnp.concatenate([lonin[a, level], cornerin[a, level]], 0)
            edge[a, level] = dot(fill[...], edge_in).astype(BF16)
        for strip in range(3):
            for g, runs in enumerate(groups(strip)):
                cells = windows_of(a, strip, g)
                cells += [latin[a, lev, c * 4 : (c + n) * 4, :] for lev, c, n in runs]
                whole = dot(place[...], jnp.concatenate(cells, 0)).astype(BF16)
                at = 0
                for lev, c, n in runs:
                    keep = min(n, max(0, 30 - c))
                    if keep:
                        own[a, lev, c * 24 : (c + keep) * 24, :] = whole[at * 24 : (at + keep) * 24]
                    at += n
    stores = []
    for a, ref in enumerate((out, dtok)):
        stores.append(
            pltpu.make_async_copy(own.at[a, :, 0:720], ref.at[:, 144:864], local.at[2 * a])
        )
        stores.append(pltpu.make_async_copy(edge.at[a], ref.at[:, 0:144], local.at[2 * a + 1]))
    for copy in stores:
        copy.start()

    for copy in stage2:
        copy.wait()
    left = s2a[yl, yh]
    right = s2b[z]
    for d in range(3):
        left = left + r2a[d]
        right = right + r2b[d]
    for k in range(4):
        s3[k, 0:4, :] = left[4 * k : 4 * k + 4]
        s3[k, 4:8, :] = right[4 * k : 4 * k + 4]
    stage3 = []
    for d in range(3):
        stage3.append(remote(s3.at[xs[d]], r3.at[d], xdev[d]))
        stage3[-1].start()
    for copy in stage3:
        copy.wait()
    total = s3[x] + r3[0] + r3[1] + r3[2]
    dqkv[:, 0:1024] = total[0:4]
    dqkv[:, 1024:1536] = total[4:8, 0:512]
    dwo[...] = total[4:8, 512:1024]
    for copy in stores:
        copy.wait()


def per_device(tokens, gain, qkv_weight, out_weight, cotangent):
    by_column = lambda a: a.transpose(0, 2, 1, 3).reshape(2, 864, D)
    vmem = pl.BlockSpec(memory_space=pltpu.VMEM)
    hbm = pl.BlockSpec(memory_space=pl.ANY)
    shape = jax.ShapeDtypeStruct
    buf = lambda *dims: pltpu.VMEM(dims, BF16)
    buf32 = lambda *dims: pltpu.VMEM(dims, F32)
    consts = tables()
    copies = 6 + 2 + 6 + 6 + 6 + 3
    out, dtok, dqkv, dwo = pl.pallas_call(
        kernel,
        out_shape=(
            shape((2, 864, D), BF16),
            shape((2, 864, D), BF16),
            shape((4, 3 * D), F32),
            shape((4, D), F32),
        ),
        in_specs=[hbm, hbm] + [vmem] * (3 + len(consts)),
        out_specs=(hbm, hbm, vmem, vmem),
        scratch_shapes=[
            buf(2, 2, 864, D),
            buf(2, 2, 144, D),
            buf(2, 2, 144, D),
            buf(2, 2, 32, D),
            buf(2, 2, 144, D),
            buf(2, 2, 864, D),
            buf(2, 2, 144, D),
            buf(2, 2, 144, D),
            buf(2, 2, 144, D),
            buf(2, 2, 32, D),
            buf(CELLS, D),
            buf(CELLS, D),
            buf(CELLS, D),
            buf(D, CELLS),
            buf(D, CELLS),
            buf32(CELLS, 1),
            buf32(CELLS, 1),
            buf(CELLS, 3 * D),
            buf(CELLS, D),
            buf(CELLS, D),
            buf(CELLS, 3 * D),
            buf32(WIN, 384),
            buf(WIN, 1152),
            buf(WIN, 1152),
            buf32(8, 2, 32, 2048),
            buf32(8, 32, 2048),
            buf(4, 2, 32, 1024),
            buf(3, 2, 32, 1024),
            buf(2, 2, 4, 16, 1024),
            buf(3, 4, 16, 1024),
            buf32(2, 2, 16, 1024),
            buf32(3, 16, 1024),
            buf32(4, 16, 1024),
            buf32(3, 16, 1024),
            buf32(4, 8, 1024),
            buf32(3, 8, 1024),
            pltpu.SemaphoreType.DMA((4,)),
            pltpu.SemaphoreType.DMA((copies,)),
            pltpu.SemaphoreType.DMA((copies,)),
        ],
        compiler_params=pltpu.CompilerParams(
            collective_id=0, has_side_effects=True, vmem_limit_bytes=60 * 2**20
        ),
        name="block",
    )(
        by_column(tokens),
        by_column(cotangent),
        gain.reshape(1, D),
        qkv_weight,
        out_weight,
        *consts,
    )
    in_place = lambda a: a.reshape(2, 36, 24, D).transpose(0, 2, 1, 3)
    return in_place(out), in_place(dtok), dqkv, dwo


def solution(mesh):
    in_specs = (P(None, "lat", "lon", None), P(), P(), P(), P(None, "lat", "lon", None))
    out_specs = (
        P(None, "lat", "lon", None),
        P(None, "lat", "lon", None),
        P(("lon", "lat"), None),
        P(("lon", "lat"), None),
    )
    return jax.shard_map(
        per_device, mesh=mesh, in_specs=in_specs, out_specs=out_specs, check_vma=False
    )
```

```python
import functools
import math

import jax
import jax.numpy as jnp
import numpy as np
from jax import lax
from jax.experimental import pallas as pl
from jax.experimental.pallas import tpu as pltpu
from jax.sharding import PartitionSpec as P

F32, BF16 = jnp.float32, jnp.bfloat16
MESH = pl.DeviceIdType.MESH
D = 512
HEAD = 32
CELLS = 1728
WIN = 144
EPS = 1e-5
NN = (((1,), (0,)), ((), ()))
NT = (((1,), (1,)), ((), ()))
TN = (((0,), (0,)), ((), ()))
SCALE = HEAD**-0.5
SCALE_LOG2E = SCALE * math.log2(math.e)


def dot(a, b, dims=NN):
    return lax.dot_general(a, b, dims, preferred_element_type=F32)


def tables():
    order = np.zeros((192, 224), np.float32)
    place = np.zeros((192, 224), np.float32)
    squeeze = np.zeros((32, 192), np.float32)
    late = np.zeros((32, 48), np.float32)
    fill = np.zeros((144, 176), np.float32)
    for c in range(8):
        for rho in range(24):
            cell = (rho // 6) * 48 + c * 6 + rho % 6
            if rho < 21:
                order[cell, c * 24 + 3 + rho] = 1
                place[c * 24 + 3 + rho, cell] = 1
            else:
                order[cell, 192 + c * 4 + rho - 21] = 1
                place[c * 24 + rho - 21, 192 + c * 4 + rho - 21] = 1
                late[c * 4 + rho - 21, c * 6 + rho % 6] = 1
                squeeze[c * 4 + rho - 21, c * 24 + rho - 21] = 1
    for c in range(6):
        for row in range(24):
            fill[c * 24 + row, c * 24 + row if row >= 3 else 144 + 8 + c * 4 + row] = 1
    heads = np.zeros((128, 256), np.float32)
    for h in range(8):
        heads[16 * h : 16 * h + 16, 32 * h : 32 * h + 32] = 1
    bf = [jnp.asarray(t, BF16) for t in (order, place, squeeze, late, fill, heads)]
    return bf + [jnp.asarray(heads, F32)]


def groups(strip):
    c = 12 * strip
    return [[(0, c, 8)], [(0, c + 8, 4), (1, c, 4)], [(1, c + 4, 8)]]


def slot(strip, i):
    if strip < 2:
        return strip * 3 + i if i < 3 else 6 + strip
    return 8 + i


def masked_tail(x, hm):
    return jnp.concatenate([x[128:144]] * 8, 0) * hm[...]


def diagonal(ref, x, hm):
    for h in range(8):
        at = slice(128 * (h // 4), 128 * (h // 4) + 128)
        mask = jnp.concatenate([hm[16 * h : 16 * h + 16, at]] * 8, 0)
        ref[128 * h : 128 * h + 128, at] = x[:128, at] * mask
    ref[1024:1152, :] = masked_tail(x, hm)


def diagonal_t(ref, x, hm):
    turned = x[:128].T
    for h in range(8):
        ref[32 * h : 32 * h + 32, 128 * h : 128 * h + 128] = turned[32 * h : 32 * h + 32]
    ref[:, 1024:1152] = masked_tail(x, hm).T


def by_query(dst, src):
    for h in range(8):
        at = slice(128 * h, 128 * h + 128)
        dst[:, at] = src[0:128, at].T
    ends = [src[128:144, 128 * h : 128 * h + 128] for h in range(8)]
    dst[:, 1024:1152] = jnp.concatenate(ends, 0).T


def last_queries(src, x, hmf):
    each = dot(src[:, 1024:1152], x, TN) * hmf[...]
    return each.reshape(8, 16, 256).sum(0)


def attend(w, lo, proj, datt, bias, hm, hmf, att, dproj, bufs):
    qt, dt, sc, dw, pt, gt, pq, gq, qd, dd, kd, vd = bufs
    rows = pl.ds(pl.multiple_of(w * WIN, 16), WIN)
    cols = lambda off: pl.ds(pl.multiple_of(off + lo, 256), 256)
    q, k, v = proj[rows, cols(0)], proj[rows, cols(512)], proj[rows, cols(1024)]
    da = datt[rows, cols(0)]
    diagonal_t(qt, q, hm)
    diagonal_t(dt, da, hm)
    sc[...] = dot(k, qt[...])
    dw[...] = dot(v, dt[...])
    for c in range(9):
        at = slice(128 * c, 128 * c + 128)
        s = sc[:, at] + (bias[:, :128] if c < 8 else bias[:, 128:256])
        d = dw[:, at]
        e = jnp.exp2((s - jnp.max(s, 0, keepdims=True)) * SCALE_LOG2E)
        p = e * (1.0 / jnp.sum(e, 0, keepdims=True))
        pt[:, at] = p.astype(BF16)
        gt[:, at] = (p * (d - jnp.sum(p * d, 0, keepdims=True)) * SCALE).astype(BF16)
    diagonal(dd, da, hm)
    dproj[rows, cols(1024)] = dot(pt[...], dd[...]).astype(BF16)
    by_query(pq, pt)
    diagonal(vd, v, hm)
    a = jnp.concatenate([dot(pq[...], vd[...]), last_queries(pt, v, hmf)], 0)
    att[rows, cols(0)] = a.astype(BF16)
    diagonal(qd, q, hm)
    dproj[rows, cols(512)] = dot(gt[...], qd[...]).astype(BF16)
    by_query(gq, gt)
    diagonal(kd, k, hm)
    dq = jnp.concatenate([dot(gq[...], kd[...]), last_queries(gt, k, hmf)], 0)
    dproj[rows, cols(0)] = dq.astype(BF16)


def kernel(
    tok, cot, gain, wqkv, wo, order, place, squeeze, late, fill, hm, hmf,
    out, dtok, dqkv, dwo,
    own, edge, halo, corner, lsend, region, lout, lonin, latin, cornerin,
    tw, cw, hid, hidt, attt, inv, mean, proj, datt, att, dproj, bias, *more,
):
    bufs, more = more[:12], more[12:]
    sums = (more[:12], more[12:24])
    local, send, recv = more[24:]
    lon, lat = lax.axis_index("lon"), lax.axis_index("lat")
    lons, lats = lax.axis_size("lon"), lax.axis_size("lat")
    z, yl, core = lon // 4, (lon // 2) % 2, lon % 2
    yh, x = lat // 4, lat % 4
    west, east = (lon + lons - 1) % lons, (lon + 1) % lons
    south, north = (lat + lats - 1) % lats, (lat + 1) % lats
    dev = lambda a, b: {"lon": a, "lat": b}
    flip = lambda bit: 1 - bit
    twin = dev(z * 4 + yl * 2 + flip(core), lat)
    zs = [(z + d) % 4 for d in (1, 2, 3)]
    xs = [(x + d) % 4 for d in (1, 2, 3)]
    ys = [(flip(yl), yh), (yl, flip(yh)), (flip(yl), flip(yh))]
    zdev = [dev(a * 4 + yl * 2 + core, lat) for a in zs]
    ydev = [dev(z * 4 + a * 2 + core, b * 4 + x) for a, b in ys]
    xdev = [dev(lon, yh * 4 + a) for a in xs]

    loads = []
    for a, ref in enumerate((tok, cot)):
        loads.append(
            pltpu.make_async_copy(ref.at[:, 144:864], own.at[a, :, 0:720], local.at[2 * a])
        )
        loads.append(pltpu.make_async_copy(ref.at[:, 0:144], edge.at[a], local.at[2 * a + 1]))
    for copy in loads:
        copy.start()
    barrier = pltpu.get_barrier_semaphore()
    halo_devs = [dev(west, lat), dev(lon, south), dev(west, south)]
    halo_devs += [dev(east, lat), dev(lon, north), dev(east, north)]
    for target in halo_devs + [twin] + zdev + ydev + xdev:
        pl.semaphore_signal(barrier, inc=1, device_id=target, device_id_type=MESH)

    used = [0]

    def remote(src, dst, target):
        n = used[0]
        used[0] += 1
        return pltpu.make_async_remote_copy(
            src_ref=src,
            dst_ref=dst,
            send_sem=send.at[n],
            recv_sem=recv.at[n],
            device_id=target,
            device_id_type=MESH,
        )

    halo_in, halo_out = [], []
    for a, ref in enumerate((tok, cot)):
        halo_in.append(remote(ref.at[:, 0:144], own.at[a, :, 720:864], dev(west, lat)))
        halo_in.append(remote(lsend.at[a, :, 0:128], halo.at[a, :, 0:128], dev(lon, south)))
        halo_in.append(remote(lsend.at[a, :, 112:144], corner.at[a], dev(west, south)))
        halo_out.append(remote(region.at[a, :, 144:288], lonin.at[a], dev(east, lat)))
        halo_out.append(remote(lout.at[a, :, 0:128], latin.at[a, :, 0:128], dev(lon, north)))
        halo_out.append(remote(lout.at[a, :, 112:144], cornerin.at[a], dev(east, north)))

    for n in (0, 1, 8, 9, 10, 11):
        bufs[n][...] = jnp.zeros_like(bufs[n])
    latin[:, :, 128:144, :] = jnp.zeros((2, 2, 16, D), BF16)

    class Scatter:
        def __init__(self, refs, w):
            (self.gw, self.r0, self.s1a, self.r1a, self.s1b, self.r1b,
             self.s2a, self.r2a, self.s2b, self.r2b, self.s3, self.r3) = refs
            self.left, self.right = slice(0, w), slice(w, 2 * w)
            self.cores = [
                remote(self.gw.at[:, flip(core), :, c], self.r0.at[:, :, c], twin)
                for c in (self.left, self.right)
            ]
            d3 = range(3)
            self.one_a = [remote(self.s1a.at[zs[d]], self.r1a.at[d], zdev[d]) for d in d3]
            self.one_b = [remote(self.s1b.at[ys[d]], self.r1b.at[d], ydev[d]) for d in d3]
            self.two_a = [remote(self.s2a.at[ys[d]], self.r2a.at[d], ydev[d]) for d in d3]
            self.two_b = [remote(self.s2b.at[zs[d]], self.r2b.at[d], zdev[d]) for d in d3]
            self.three = [remote(self.s3.at[xs[d]], self.r3.at[d], xdev[d]) for d in d3]

        def put(self, lo, grad):
            grad_scale = 1.0 / math.sqrt(CELLS * 128)
            self.gw[:, :, :, lo : lo + 256] = (grad * grad_scale).reshape(8, 2, 32, 256)

        def step1(self):
            self.cores[0].wait()
            for k in range(8):
                total = self.gw[k, core, :, self.left] + self.r0[k, :, self.left]
                self.gw[k, core, :, self.left] = total
                self.s1a[k // 2, k % 2] = total.astype(BF16)
            for copy in self.one_a:
                copy.start()
            self.cores[1].wait()
            for k in range(8):
                total = self.gw[k, core, :, self.right] + self.r0[k, :, self.right]
                self.gw[k, core, :, self.right] = total
                low = total.astype(BF16)
                for h in range(2):
                    self.s1b[k % 2, h, k // 2] = low[16 * h : 16 * h + 16]
            for copy in self.one_b:
                copy.start()

        def step2(self):
            for copy in self.one_a:
                copy.wait()
            for k in range(2):
                total = self.gw[z * 2 + k, core, :, self.left]
                for d in range(3):
                    total = total + self.r1a[d, k].astype(F32)
                for h in range(2):
                    self.s2a[k, h] = total[16 * h : 16 * h + 16]
            for copy in self.two_a:
                copy.start()
            for copy in self.one_b:
                copy.wait()
            mine = pl.ds(pl.multiple_of(yh * 16, 16), 16)
            for k in range(4):
                total = self.gw[k * 2 + yl, core, mine, self.right]
                for d in range(3):
                    total = total + self.r1b[d, k].astype(F32)
                self.s2b[k] = total
            for copy in self.two_b:
                copy.start()

        def step3(self):
            for copy in self.two_a + self.two_b:
                copy.wait()
            left, right = self.s2a[yl, yh], self.s2b[z]
            for d in range(3):
                left = left + self.r2a[d]
                right = right + self.r2b[d]
            for k in range(4):
                self.s3[k, 0:4, :] = left[4 * k : 4 * k + 4]
                self.s3[k, 4:8, :] = right[4 * k : 4 * k + 4]
            for copy in self.three:
                copy.start()

        def result(self):
            for copy in self.three:
                copy.wait()
            total = self.s3[x] + self.r3[0] + self.r3[1] + self.r3[2]
            return jnp.concatenate([total[0:4], total[4:8]], 1)

    early, final = Scatter(sums[0], 384), Scatter(sums[1], 640)

    def gather(a, strip, g, which):
        runs = groups(strip)[g]
        cells = [own[a, lev, c * 24 : (c + n) * 24, :] for lev, c, n in runs]
        lo, hi = which
        width = 192
        if hi == 4:
            cells += [halo[a, lev, c * 4 : (c + n) * 4, :] for lev, c, n in runs]
            width = 224
        got = dot(order[48 * lo : 48 * hi, :width], jnp.concatenate(cells, 0)).astype(BF16)
        for i in range(lo, hi):
            at = slot(strip, i) * WIN + g * 48
            (tw, cw)[a][at : at + 48, :] = got[(i - lo) * 48 : (i - lo) * 48 + 48]

    def project(first):
        @pl.loop(0, 3)
        def _(t):
            rows = pl.ds(first + t * 288, 288)
            cells = tw[rows, :].astype(F32)
            mu = jnp.mean(cells, -1, keepdims=True)
            cells = cells - mu
            iv = lax.rsqrt(jnp.mean(cells * cells, -1, keepdims=True) + EPS)
            h = (cells * iv * gain[...]).astype(BF16)
            hid[rows, :] = h
            mean[rows, :] = mu
            inv[rows, :] = iv
            for n in range(3):
                at = slice(512 * n, 512 * n + 512)
                proj[rows, at] = dot(h, wqkv[:, at]).astype(BF16)
            datt[rows, :] = dot(cw[rows, :], wo[...], NT).astype(BF16)

    res = (hid, datt)

    def outputs(first):
        @pl.loop(0, 3)
        def _(t):
            rows = pl.ds(first + t * 288, 288)
            cells = tw[rows, :].astype(F32)
            res[0][rows, :] = (cells + dot(att[rows, :], wo[...])).astype(BF16)
            u = dot(dproj[rows, :], wqkv[...], NT) * gain[...]
            iv = inv[rows, :]
            normed = (cells - mean[rows, :]) * iv
            d = u - jnp.mean(u, -1, keepdims=True)
            d = d - normed * jnp.mean(u * normed, -1, keepdims=True)
            res[1][rows, :] = (cw[rows, :].astype(F32) + iv * d).astype(BF16)

    def windows_of(a, strip, g):
        at = [slot(strip, i) * WIN + g * 48 for i in range(4)]
        return [res[a][n : n + 48, :] for n in at]

    for copy in loads:
        copy.wait()
    for a in range(2):
        for strip in range(2):
            for g in range(3):
                gather(a, strip, g, (0, 3))

    def pairs_of(a, level, column, count):
        got = []
        here = min(count, max(0, 30 - column))
        if here:
            got.append(own[a, level, column * 24 : (column + here) * 24, :])
        if count - here:
            c = column + here - 30
            got.append(edge[a, level, c * 24 : (c + count - here) * 24, :])
        return got

    for a in range(2):
        for level in range(2):
            for column, count in ((0, 8), (8, 8), (16, 8), (24, 8), (32, 4)):
                cells = jnp.concatenate(pairs_of(a, level, column, count), 0)
                small = dot(squeeze[: count * 4, : count * 24], cells).astype(BF16)
                lsend[a, level, column * 4 : (column + count) * 4, :] = small
    project(0)
    pl.semaphore_wait(barrier, 16)
    for copy in halo_in:
        copy.start()

    def receive_halo():
        for copy in halo_in:
            copy.wait()
        late_row = lax.broadcasted_iota(jnp.int32, (32, D), 0) >= 8
        for a in range(2):
            for level in range(2):
                halo[a, level, 112:144, :] = jnp.where(
                    late_row, corner[a, level], halo[a, level, 112:144, :]
                )
            for g in range(3):
                for strip in range(2):
                    gather(a, strip, g, (3, 4))
                gather(a, 2, g, (0, 4))
        project(864)

    def return_halo():
        hidt[...] = hid[...].T
        outputs(864)
        for a in range(2):
            for strip in range(3):
                for g, runs in enumerate(groups(strip)):
                    if strip == 2:
                        cells = windows_of(a, strip, g)
                        whole = dot(place[:, :192], jnp.concatenate(cells, 0)).astype(BF16)
                    at = slot(strip, 3) * WIN + g * 48
                    small = dot(late[...], res[a][at : at + 48, :]).astype(BF16)
                    at = 0
                    for lev, c, n in runs:
                        lout[a, lev, c * 4 : (c + n) * 4, :] = small[at * 4 : (at + n) * 4]
                        if strip == 2:
                            to = slice((c - 24) * 24, (c - 24 + n) * 24)
                            region[a, lev, to, :] = whole[at * 24 : (at + n) * 24]
                        at += n
            for copy in halo_out[3 * a : 3 * a + 3]:
                copy.start()
        for n in range(3):
            early.put(256 * n, dot(hidt[...], dproj[:, 512 * n : 512 * n + 256]))
            if n:
                early.cores[n - 1].start()

    @pl.loop(0, 4)
    def _(part):
        pl.when(part == 1)(receive_halo)
        pl.when(part == 3)(return_halo)
        lo = jnp.where(part >= 2, 256, 0)
        first = jnp.where(jnp.logical_or(part == 1, part == 2), 6, 0)
        key_side = (lax.broadcasted_iota(jnp.int32, (WIN, 1), 0) % 6) >= 3
        lane = lax.broadcasted_iota(jnp.int32, (1, 256), 1)
        query = jnp.where(lane < 128, lane, 128 + lane % 16)
        differ = key_side != ((query % 6) >= 3)

        @pl.loop(0, 6)
        def _(i):
            w = first + i
            last = jnp.logical_or(jnp.logical_or(w == 6, w == 7), w == 11)
            apart = jnp.logical_and(last, lat == lats - 1)
            bias[...] = jnp.where(jnp.logical_and(apart, differ), -1e30, 0.0)
            attend(w, lo, proj, datt, bias, hm, hmf, att, dproj, bufs)
            pl.when(jnp.logical_and(part == 3, i == 1))(early.step1)

    attt[...] = att[...].T
    for n in range(5):
        if n < 3:
            grad = dot(hidt[...], dproj[:, 512 * n + 256 : 512 * n + 512])
        else:
            grad = dot(attt[...], cw[:, 256 * n - 768 : 256 * n - 512])
        final.put(256 * n, grad)
        if n in (2, 4):
            final.cores[n // 2 - 1].start()
    early.step2()
    outputs(0)
    final.step1()
    early.step3()

    for copy in halo_out:
        copy.wait()
    for a in range(2):
        for level in range(2):
            edge_in = jnp.concatenate([lonin[a, level], cornerin[a, level]], 0)
            edge[a, level] = dot(fill[...], edge_in).astype(BF16)
        for strip in range(3):
            for g, runs in enumerate(groups(strip)):
                cells = windows_of(a, strip, g)
                cells += [latin[a, lev, c * 4 : (c + n) * 4, :] for lev, c, n in runs]
                whole = dot(place[...], jnp.concatenate(cells, 0)).astype(BF16)
                at = 0
                for lev, c, n in runs:
                    keep = min(n, max(0, 30 - c))
                    if keep:
                        own[a, lev, c * 24 : (c + keep) * 24, :] = whole[at * 24 : (at + keep) * 24]
                    at += n
    stores = []
    for a, ref in enumerate((out, dtok)):
        stores.append(
            pltpu.make_async_copy(own.at[a, :, 0:720], ref.at[:, 144:864], local.at[2 * a])
        )
        stores.append(pltpu.make_async_copy(edge.at[a], ref.at[:, 0:144], local.at[2 * a + 1]))
    for copy in stores:
        copy.start()

    grads = early.result()
    for n in range(3):
        dqkv[:, 512 * n : 512 * n + 256] = grads[:, 256 * n : 256 * n + 256]
    final.step2()
    final.step3()
    grads = final.result()
    for n in range(3):
        dqkv[:, 512 * n + 256 : 512 * n + 512] = grads[:, 256 * n : 256 * n + 256]
    dwo[...] = grads[:, 768:1280]
    for copy in stores:
        copy.wait()


def per_device(tokens, gain, qkv_weight, out_weight, cotangent):
    by_column = lambda a: a.transpose(0, 2, 1, 3).reshape(2, 864, D)
    vmem = pl.BlockSpec(memory_space=pltpu.VMEM)
    hbm = pl.BlockSpec(memory_space=pl.ANY)
    shape = jax.ShapeDtypeStruct
    buf = lambda *dims: pltpu.VMEM(dims, BF16)
    buf32 = lambda *dims: pltpu.VMEM(dims, F32)
    consts = tables()
    copies = 12 + 2 * (2 + 6 + 6 + 3)

    def scatter(w):
        return [
            buf32(8, 2, 32, 2 * w),
            buf32(8, 32, 2 * w),
            buf(4, 2, 32, w),
            buf(3, 2, 32, w),
            buf(2, 2, 4, 16, w),
            buf(3, 4, 16, w),
            buf32(2, 2, 16, w),
            buf32(3, 16, w),
            buf32(4, 16, w),
            buf32(3, 16, w),
            buf32(4, 8, w),
            buf32(3, 8, w),
        ]

    out, dtok, dqkv, dwo = pl.pallas_call(
        kernel,
        out_shape=(
            shape((2, 864, D), BF16),
            shape((2, 864, D), BF16),
            shape((4, 3 * D), F32),
            shape((4, D), F32),
        ),
        in_specs=[hbm, hbm] + [vmem] * (3 + len(consts)),
        out_specs=(hbm, hbm, vmem, vmem),
        scratch_shapes=[
            buf(2, 2, 864, D),
            buf(2, 2, 144, D),
            buf(2, 2, 144, D),
            buf(2, 2, 32, D),
            buf(2, 2, 144, D),
            buf(2, 2, 288, D),
            buf(2, 2, 144, D),
            buf(2, 2, 144, D),
            buf(2, 2, 144, D),
            buf(2, 2, 32, D),
            buf(CELLS, D),
            buf(CELLS, D),
            buf(CELLS, D),
            buf(D, CELLS),
            buf(D, CELLS),
            buf32(CELLS, 1),
            buf32(CELLS, 1),
            buf(CELLS, 3 * D),
            buf(CELLS, D),
            buf(CELLS, D),
            buf(CELLS, 3 * D),
            buf32(WIN, 256),
            *[buf(256, 1152)] * 2,
            *[buf32(WIN, 1152)] * 2,
            *[buf(WIN, 1152)] * 2,
            *[buf(128, 1152)] * 2,
            *[buf(1152, 256)] * 4,
            *scatter(384),
            *scatter(640),
            pltpu.SemaphoreType.DMA((4,)),
            pltpu.SemaphoreType.DMA((copies,)),
            pltpu.SemaphoreType.DMA((copies,)),
        ],
        compiler_params=pltpu.CompilerParams(
            collective_id=0, has_side_effects=True, vmem_limit_bytes=60 * 2**20
        ),
        name="block",
    )(
        by_column(tokens),
        by_column(cotangent),
        gain.reshape(1, D),
        qkv_weight,
        out_weight,
        *consts,
    )
    in_place = lambda a: a.reshape(2, 36, 24, D).transpose(0, 2, 1, 3)
    return in_place(out), in_place(dtok), dqkv, dwo


def solution(mesh):
    in_specs = (P(None, "lat", "lon", None), P(), P(), P(), P(None, "lat", "lon", None))
    out_specs = (
        P(None, "lat", "lon", None),
        P(None, "lat", "lon", None),
        P(("lon", "lat"), None),
        P(("lon", "lat"), None),
    )
    return jax.shard_map(
        per_device, mesh=mesh, in_specs=in_specs, out_specs=out_specs, check_vma=False
    )
```

```python
import functools
import math

import jax
import jax.numpy as jnp
import numpy as np
from jax import lax
from jax.experimental import pallas as pl
from jax.experimental.pallas import tpu as pltpu
from jax.sharding import PartitionSpec as P

F32, BF16 = jnp.float32, jnp.bfloat16
MESH = pl.DeviceIdType.MESH
D = 512
HEAD = 32
CELLS = 1728
WIN = 144
EPS = 1e-5
NN = (((1,), (0,)), ((), ()))
NT = (((1,), (1,)), ((), ()))
TN = (((0,), (0,)), ((), ()))
SCALE = HEAD**-0.5
SCALE_LOG2E = SCALE * math.log2(math.e)


def dot(a, b, dims=NN):
    return lax.dot_general(a, b, dims, preferred_element_type=F32)


def groups(strip):
    c = 12 * strip
    return [[(0, c, 8)], [(0, c + 8, 4), (1, c, 4)], [(1, c + 4, 8)]]


def tables():
    order = np.zeros((192, 192), np.float32)
    squeeze = np.zeros((48, 384), np.float32)
    last = np.zeros((432, 240), np.float32)
    spread = np.zeros((480, 192), np.float32)
    for c in range(8):
        for rho in range(21):
            order[(rho // 6) * 48 + c * 6 + rho % 6, c * 24 + 3 + rho] = 1
    for c in range(16):
        for r in range(3):
            squeeze[c * 3 + r, c * 24 + r] = 1
    for c in range(60):
        for r in range(3):
            spread[c * 8 + r, c * 3 + r] = 1
    for strip in range(3):
        for g, runs in enumerate(groups(strip)):
            pairs = [(lev, c + i) for lev, c, n in runs for i in range(n)]
            for p, (lev, c) in enumerate(pairs):
                at = (lev * 30 + c) * 3 if c < 30 else 192 + (lev * 6 + c - 30) * 3
                for r in range(3):
                    last[strip * 144 + g * 48 + p * 6 + 3 + r, at + r] = 1
    heads = np.zeros((128, 256), np.float32)
    for h in range(8):
        heads[16 * h : 16 * h + 16, 32 * h : 32 * h + 32] = 1
    bf = [jnp.asarray(t, BF16) for t in (order, order.T, squeeze, last, last.T, spread, heads)]
    return bf + [jnp.asarray(heads, F32)]


def slot(strip, i):
    if i == 3:
        return 9 + strip
    return strip * 3 + i


def masked_tail(x, hm):
    return jnp.concatenate([x[128:144]] * 8, 0) * hm[...]


def diagonal(ref, x, hm):
    for h in range(8):
        at = slice(128 * (h // 4), 128 * (h // 4) + 128)
        mask = jnp.concatenate([hm[16 * h : 16 * h + 16, at]] * 8, 0)
        ref[128 * h : 128 * h + 128, at] = x[:128, at] * mask
    ref[1024:1152, :] = masked_tail(x, hm)


def diagonal_t(ref, x, hm):
    turned = x[:128].T
    for h in range(8):
        ref[32 * h : 32 * h + 32, 128 * h : 128 * h + 128] = turned[32 * h : 32 * h + 32]
    ref[:, 1024:1152] = masked_tail(x, hm).T


def by_query(dst, src):
    for h in range(8):
        at = slice(128 * h, 128 * h + 128)
        dst[:, at] = src[0:128, at].T
    ends = [src[128:144, 128 * h : 128 * h + 128] for h in range(8)]
    dst[:, 1024:1152] = jnp.concatenate(ends, 0).T


def last_queries(src, x, hmf):
    each = dot(src[:, 1024:1152], x, TN) * hmf[...]
    return each.reshape(8, 16, 256).sum(0)


def attend(w, lo, proj, datt, bias, hm, hmf, att, dproj, bufs):
    qt, dt, sc, dw, pt, gt, pq, gq, qd, dd, kd, vd = bufs
    rows = pl.ds(pl.multiple_of(w * WIN, 16), WIN)
    cols = lambda off: pl.ds(pl.multiple_of(off + lo, 256), 256)
    q, k, v = proj[rows, cols(0)], proj[rows, cols(512)], proj[rows, cols(1024)]
    da = datt[rows, cols(0)]
    diagonal_t(qt, q, hm)
    diagonal_t(dt, da, hm)
    sc[...] = dot(k, qt[...])
    dw[...] = dot(v, dt[...])
    for c in range(9):
        at = slice(128 * c, 128 * c + 128)
        s = sc[:, at] + (bias[:, :128] if c < 8 else bias[:, 128:256])
        d = dw[:, at]
        e = jnp.exp2((s - jnp.max(s, 0, keepdims=True)) * SCALE_LOG2E)
        p = e * (1.0 / jnp.sum(e, 0, keepdims=True))
        pt[:, at] = p.astype(BF16)
        gt[:, at] = (p * (d - jnp.sum(p * d, 0, keepdims=True)) * SCALE).astype(BF16)
    diagonal(dd, da, hm)
    dproj[rows, cols(1024)] = dot(pt[...], dd[...]).astype(BF16)
    by_query(pq, pt)
    diagonal(vd, v, hm)
    a = jnp.concatenate([dot(pq[...], vd[...]), last_queries(pt, v, hmf)], 0)
    att[rows, cols(0)] = a.astype(BF16)
    diagonal(qd, q, hm)
    dproj[rows, cols(512)] = dot(gt[...], qd[...]).astype(BF16)
    by_query(gq, gt)
    diagonal(kd, k, hm)
    dq = jnp.concatenate([dot(gq[...], kd[...]), last_queries(gt, k, hmf)], 0)
    dproj[rows, cols(0)] = dq.astype(BF16)


def kernel(
    tok, cot, gain, wqkv, wo, order, place, squeeze, late, late_t, spread, hm, hmf,
    out, dtok, dqkv, dwo,
    own, edge, halo, lsend, region, lout, lonin, latin,
    tw, cw, hid, hidt, attt, inv, mean, proj, datt, att, dproj, bias, *more,
):
    bufs, more = more[:12], more[12:]
    sums = (more[:13], more[13:26])
    local, send, recv = more[26:]
    lon, lat = lax.axis_index("lon"), lax.axis_index("lat")
    lons, lats = lax.axis_size("lon"), lax.axis_size("lat")
    z, yl, core = lon // 4, (lon // 2) % 2, lon % 2
    yh, x = lat // 4, lat % 4
    west, east = (lon + lons - 1) % lons, (lon + 1) % lons
    south, north = (lat + lats - 1) % lats, (lat + 1) % lats
    dev = lambda a, b: {"lon": a, "lat": b}
    flip = lambda bit: 1 - bit
    twin = dev(z * 4 + yl * 2 + flip(core), lat)
    zs = [(z + d) % 4 for d in (1, 2, 3)]
    xs = [(x + d) % 4 for d in (1, 2, 3)]
    ys = [(flip(yl), yh), (yl, flip(yh)), (flip(yl), flip(yh))]
    zdev = [dev(a * 4 + yl * 2 + core, lat) for a in zs]
    ydev = [dev(z * 4 + a * 2 + core, b * 4 + x) for a, b in ys]
    xdev = [dev(lon, yh * 4 + a) for a in xs]

    loads = []
    for a, ref in enumerate((tok, cot)):
        loads.append(
            pltpu.make_async_copy(ref.at[:, 144:864], own.at[a, :, 0:720], local.at[2 * a])
        )
        loads.append(pltpu.make_async_copy(ref.at[:, 0:144], edge.at[a], local.at[2 * a + 1]))
    for copy in loads:
        copy.start()
    barrier = pltpu.get_barrier_semaphore()
    halo_devs = [dev(west, lat), dev(lon, south), dev(west, south)]
    halo_devs += [dev(east, lat), dev(lon, north), dev(east, north)]
    for target in halo_devs + [twin] + zdev + ydev + xdev:
        pl.semaphore_signal(barrier, inc=1, device_id=target, device_id_type=MESH)

    used = [0]

    def remote(src, dst, target):
        n = used[0]
        used[0] += 1
        return pltpu.make_async_remote_copy(
            src_ref=src,
            dst_ref=dst,
            send_sem=send.at[n],
            recv_sem=recv.at[n],
            device_id=target,
            device_id_type=MESH,
        )

    halo_in, halo_out = [], []
    for a, ref in enumerate((tok, cot)):
        halo_in.append(remote(ref.at[:, 0:144], own.at[a, :, 720:864], dev(west, lat)))
        halo_out.append(remote(region.at[a, :, 144:288], lonin.at[a], dev(east, lat)))
    for a in range(2):
        for rows, lon_in, lon_out in ((slice(0, 192), lon, lon), (slice(192, 240), west, east)):
            halo_in.append(remote(lsend.at[a, rows], halo.at[a, rows], dev(lon_in, south)))
            halo_out.append(remote(lout.at[a, rows], latin.at[a, rows], dev(lon_out, north)))

    for n in (0, 1, 8, 9, 10, 11):
        bufs[n][...] = jnp.zeros_like(bufs[n])

    class Scatter:
        def __init__(self, refs, w):
            (self.gw, self.s0, self.r0, self.s1a, self.r1a, self.s1b, self.r1b,
             self.s2a, self.r2a, self.s2b, self.r2b, self.s3, self.r3) = refs
            self.left, self.right = slice(0, w), slice(w, 2 * w)
            self.cores = [
                remote(self.s0.at[:, :, c], self.r0.at[:, :, c], twin)
                for c in (self.left, self.right)
            ]
            d3 = range(3)
            self.one_a = [remote(self.s1a.at[zs[d]], self.r1a.at[d], zdev[d]) for d in d3]
            self.one_b = [remote(self.s1b.at[ys[d]], self.r1b.at[d], ydev[d]) for d in d3]
            self.two_a = [remote(self.s2a.at[ys[d]], self.r2a.at[d], ydev[d]) for d in d3]
            self.two_b = [remote(self.s2b.at[zs[d]], self.r2b.at[d], zdev[d]) for d in d3]
            self.three = [remote(self.s3.at[xs[d]], self.r3.at[d], xdev[d]) for d in d3]

        def put(self, lo, grad):
            grad_scale = 1.0 / math.sqrt(CELLS * 128)
            grad = (grad * grad_scale).reshape(8, 2, 32, 256)
            one, two = grad[:, 0], grad[:, 1]
            self.gw[:, :, lo : lo + 256] = jnp.where(core == 0, one, two)
            self.s0[:, :, lo : lo + 256] = jnp.where(core == 0, two, one).astype(BF16)

        def step1(self):
            self.cores[0].wait()
            for k in range(8):
                total = self.gw[k, :, self.left] + self.r0[k, :, self.left].astype(F32)
                self.gw[k, :, self.left] = total
                self.s1a[k // 2, k % 2] = total.astype(BF16)
            for copy in self.one_a:
                copy.start()
            self.cores[1].wait()
            for k in range(8):
                total = self.gw[k, :, self.right] + self.r0[k, :, self.right].astype(F32)
                self.gw[k, :, self.right] = total
                low = total.astype(BF16)
                for h in range(2):
                    self.s1b[k % 2, h, k // 2] = low[16 * h : 16 * h + 16]
            for copy in self.one_b:
                copy.start()

        def step2(self):
            for copy in self.one_a:
                copy.wait()
            for k in range(2):
                total = self.gw[z * 2 + k, :, self.left]
                for d in range(3):
                    total = total + self.r1a[d, k].astype(F32)
                for h in range(2):
                    self.s2a[k, h] = total[16 * h : 16 * h + 16]
            for copy in self.two_a:
                copy.start()
            for copy in self.one_b:
                copy.wait()
            mine = pl.ds(pl.multiple_of(yh * 16, 16), 16)
            for k in range(4):
                total = self.gw[k * 2 + yl, mine, self.right]
                for d in range(3):
                    total = total + self.r1b[d, k].astype(F32)
                self.s2b[k] = total
            for copy in self.two_b:
                copy.start()

        def step3(self):
            for copy in self.two_a + self.two_b:
                copy.wait()
            left, right = self.s2a[yl, yh], self.s2b[z]
            for d in range(3):
                left = left + self.r2a[d]
                right = right + self.r2b[d]
            for k in range(4):
                self.s3[k, 0:4, :] = left[4 * k : 4 * k + 4]
                self.s3[k, 4:8, :] = right[4 * k : 4 * k + 4]
            for copy in self.three:
                copy.start()

        def result(self):
            for copy in self.three:
                copy.wait()
            total = self.s3[x] + self.r3[0] + self.r3[1] + self.r3[2]
            return jnp.concatenate([total[0:4], total[4:8]], 1)

    early, final = Scatter(sums[0], 384), Scatter(sums[1], 640)

    def rows_of(a, strip, g):
        runs = groups(strip)[g]
        return jnp.concatenate([own[a, v, c * 24 : (c + n) * 24, :] for v, c, n in runs], 0)

    def gather(strip):
        for a in range(2):
            for g in range(3):
                got = dot(order[:144, :], rows_of(a, strip, g)).astype(BF16)
                for i in range(3):
                    at = slot(strip, i) * WIN + g * 48
                    (tw, cw)[a][at : at + 48, :] = got[i * 48 : i * 48 + 48]

    def project(first, chunks):
        @pl.loop(0, chunks)
        def _(t):
            rows = pl.ds(pl.multiple_of(first + t * 432, 16), 432)
            cells = tw[rows, :].astype(F32)
            mu = jnp.mean(cells, -1, keepdims=True)
            cells = cells - mu
            iv = lax.rsqrt(jnp.mean(cells * cells, -1, keepdims=True) + EPS)
            h = (cells * iv * gain[...]).astype(BF16)
            hid[rows, :] = h
            mean[rows, :] = mu
            inv[rows, :] = iv
            for n in range(3):
                at = slice(512 * n, 512 * n + 512)
                proj[rows, at] = dot(h, wqkv[:, at]).astype(BF16)
            datt[rows, :] = dot(cw[rows, :], wo[...], NT).astype(BF16)

    res = (hid, datt)

    def outputs(first):
        @pl.loop(0, 2)
        def _(t):
            rows = pl.ds(pl.multiple_of(first + t * 432, 16), 432)
            cells = tw[rows, :].astype(F32)
            res[0][rows, :] = (cells + dot(att[rows, :], wo[...])).astype(BF16)
            u = dot(dproj[rows, :], wqkv[...], NT) * gain[...]
            iv = inv[rows, :]
            normed = (cells - mean[rows, :]) * iv
            d = u - jnp.mean(u, -1, keepdims=True)
            d = d - normed * jnp.mean(u * normed, -1, keepdims=True)
            res[1][rows, :] = (cw[rows, :].astype(F32) + iv * d).astype(BF16)

    def windows_of(a, strip, g):
        at = [slot(strip, i) * WIN + g * 48 for i in range(4)]
        return [res[a][n : n + 48, :] for n in at]

    for copy in loads:
        copy.wait()
    gather(0)
    gather(1)
    for a in range(2):
        lead = [own[a, 0, 0:384, :]]
        lead += [jnp.concatenate([own[a, 0, 384:720, :], own[a, 1, 0:48, :]], 0)]
        lead += [own[a, 1, 48:432, :], own[a, 1, 432:720, :]]
        lead += [jnp.concatenate([edge[a, 0], edge[a, 1]], 0)]
        for n, cells in enumerate(lead):
            small = dot(squeeze[:, : cells.shape[0]], cells).astype(BF16)
            lsend[a, 48 * n : 48 * n + 48, :] = small
    project(0, 2)
    pl.semaphore_wait(barrier, 16)
    for copy in halo_in:
        copy.start()

    def receive_columns():
        for copy in halo_in[:2]:
            copy.wait()
        gather(2)
        project(864, 1)

    def receive_rows():
        for copy in halo_in[2:]:
            copy.wait()
        for a in range(2):
            base = dot(late[...], halo[a])
            for strip in range(3):
                for g in range(3):
                    at = strip * WIN + g * 48
                    got = dot(order[144:192, :], rows_of(a, strip, g)) + base[at : at + 48]
                    (tw, cw)[a][1296 + at : 1344 + at, :] = got.astype(BF16)
        project(1296, 1)

    def first_gradients():
        hidt[...] = hid[...].T
        for n in range(3):
            early.put(256 * n, dot(hidt[...], dproj[:, 512 * n : 512 * n + 256]))
            if n:
                early.cores[n - 1].start()

    def return_halo():
        for a in range(2):
            lout[a] = dot(late_t[...], res[a][1296:1728, :]).astype(BF16)
            for g, runs in enumerate(groups(2)):
                cells = windows_of(a, 2, g)
                whole = dot(place[...], jnp.concatenate(cells, 0)).astype(BF16)
                at = 0
                for lev, c, n in runs:
                    to = slice((c - 24) * 24, (c - 24 + n) * 24)
                    region[a, lev, to, :] = whole[at * 24 : (at + n) * 24]
                    at += n
        for copy in halo_out:
            copy.start()

    @pl.loop(0, 6)
    def _(part):
        pl.when(part == 2)(receive_columns)
        pl.when(part == 4)(receive_rows)
        pl.when(part == 5)(first_gradients)
        lo = (part % 2) * 256
        first = jnp.where(part < 2, 0, jnp.where(part < 4, 6, 9))
        count = jnp.where(part < 2, 6, 3)
        key_side = (lax.broadcasted_iota(jnp.int32, (WIN, 1), 0) % 6) >= 3
        lane = lax.broadcasted_iota(jnp.int32, (1, 256), 1)
        query = jnp.where(lane < 128, lane, 128 + lane % 16)
        differ = key_side != ((query % 6) >= 3)
        apart = jnp.logical_and(part >= 4, lat == lats - 1)
        bias[...] = jnp.where(jnp.logical_and(apart, differ), -1e30, 0.0)

        @pl.loop(first, first + count)
        def _(w):
            attend(w, lo, proj, datt, bias, hm, hmf, att, dproj, bufs)

    early.step1()
    outputs(864)
    return_halo()
    attt[...] = att[...].T
    for n in range(5):
        if n < 3:
            grad = dot(hidt[...], dproj[:, 512 * n + 256 : 512 * n + 512])
        else:
            grad = dot(attt[...], cw[:, 256 * n - 768 : 256 * n - 512])
        final.put(256 * n, grad)
        if n in (2, 4):
            final.cores[n // 2 - 1].start()
    early.step2()
    outputs(0)
    final.step1()
    early.step3()
    final.step2()
    grads = early.result()
    for n in range(3):
        dqkv[:, 512 * n : 512 * n + 256] = grads[:, 256 * n : 256 * n + 256]
    final.step3()

    for copy in halo_out:
        copy.wait()

    def with_first(cells, first):
        cells = cells.reshape(-1, 24, D)
        first = first.reshape(-1, 8, D)
        cells = jnp.concatenate([cells[:, 0:8] + first, cells[:, 8:24]], 1)
        return cells.reshape(-1, D).astype(BF16)

    for a in range(2):
        rows = dot(spread[:96, :48], latin[a, 192:240, :])
        for level in range(2):
            cells = lonin[a, level].astype(F32)
            edge[a, level] = with_first(cells, rows[48 * level : 48 * level + 48])
        rows = dot(spread[...], latin[a, 0:192, :])
        for strip in range(3):
            for g, runs in enumerate(groups(strip)):
                cells = windows_of(a, strip, g)
                whole = dot(place[...], jnp.concatenate(cells, 0))
                at = 0
                for lev, c, n in runs:
                    keep = min(n, max(0, 30 - c))
                    if keep:
                        top = (lev * 30 + c) * 8
                        part = with_first(whole[at * 24 : (at + keep) * 24], rows[top : top + 8 * keep])
                        own[a, lev, c * 24 : (c + keep) * 24, :] = part
                    at += n
    stores = []
    for a, ref in enumerate((out, dtok)):
        stores.append(
            pltpu.make_async_copy(own.at[a, :, 0:720], ref.at[:, 144:864], local.at[2 * a])
        )
        stores.append(pltpu.make_async_copy(edge.at[a], ref.at[:, 0:144], local.at[2 * a + 1]))
    for copy in stores:
        copy.start()

    grads = final.result()
    for n in range(3):
        dqkv[:, 512 * n + 256 : 512 * n + 512] = grads[:, 256 * n : 256 * n + 256]
    dwo[...] = grads[:, 768:1280]
    for copy in stores:
        copy.wait()


def per_device(tokens, gain, qkv_weight, out_weight, cotangent):
    by_column = lambda a: a.transpose(0, 2, 1, 3).reshape(2, 864, D)
    vmem = pl.BlockSpec(memory_space=pltpu.VMEM)
    hbm = pl.BlockSpec(memory_space=pl.ANY)
    shape = jax.ShapeDtypeStruct
    buf = lambda *dims: pltpu.VMEM(dims, BF16)
    buf32 = lambda *dims: pltpu.VMEM(dims, F32)
    consts = tables()
    copies = 12 + 2 * (2 + 6 + 6 + 3)

    def scatter(w):
        return [
            buf32(8, 32, 2 * w),
            buf(8, 32, 2 * w),
            buf(8, 32, 2 * w),
            buf(4, 2, 32, w),
            buf(3, 2, 32, w),
            buf(2, 2, 4, 16, w),
            buf(3, 4, 16, w),
            buf32(2, 2, 16, w),
            buf32(3, 16, w),
            buf32(4, 16, w),
            buf32(3, 16, w),
            buf32(4, 8, w),
            buf32(3, 8, w),
        ]

    out, dtok, dqkv, dwo = pl.pallas_call(
        kernel,
        out_shape=(
            shape((2, 864, D), BF16),
            shape((2, 864, D), BF16),
            shape((4, 3 * D), F32),
            shape((4, D), F32),
        ),
        in_specs=[hbm, hbm] + [vmem] * (3 + len(consts)),
        out_specs=(hbm, hbm, vmem, vmem),
        scratch_shapes=[
            buf(2, 2, 864, D),
            buf(2, 2, 144, D),
            buf(2, 240, D),
            buf(2, 240, D),
            buf(2, 2, 288, D),
            buf(2, 240, D),
            buf(2, 2, 144, D),
            buf(2, 240, D),
            buf(CELLS, D),
            buf(CELLS, D),
            buf(CELLS, D),
            buf(D, CELLS),
            buf(D, CELLS),
            buf32(CELLS, 1),
            buf32(CELLS, 1),
            buf(CELLS, 3 * D),
            buf(CELLS, D),
            buf(CELLS, D),
            buf(CELLS, 3 * D),
            buf32(WIN, 256),
            *[buf(256, 1152)] * 2,
            *[buf32(WIN, 1152)] * 2,
            *[buf(WIN, 1152)] * 2,
            *[buf(128, 1152)] * 2,
            *[buf(1152, 256)] * 4,
            *scatter(384),
            *scatter(640),
            pltpu.SemaphoreType.DMA((4,)),
            pltpu.SemaphoreType.DMA((copies,)),
            pltpu.SemaphoreType.DMA((copies,)),
        ],
        compiler_params=pltpu.CompilerParams(
            collective_id=0, has_side_effects=True, vmem_limit_bytes=60 * 2**20
        ),
        name="block",
    )(
        by_column(tokens),
        by_column(cotangent),
        gain.reshape(1, D),
        qkv_weight,
        out_weight,
        *consts,
    )
    in_place = lambda a: a.reshape(2, 36, 24, D).transpose(0, 2, 1, 3)
    return in_place(out), in_place(dtok), dqkv, dwo


def solution(mesh):
    in_specs = (P(None, "lat", "lon", None), P(), P(), P(), P(None, "lat", "lon", None))
    out_specs = (
        P(None, "lat", "lon", None),
        P(None, "lat", "lon", None),
        P(("lon", "lat"), None),
        P(("lon", "lat"), None),
    )
    return jax.shard_map(
        per_device, mesh=mesh, in_specs=in_specs, out_specs=out_specs, check_vma=False
    )
```

```python
import functools
import math

import jax
import jax.numpy as jnp
import numpy as np
from jax import lax
from jax.experimental import pallas as pl
from jax.experimental.pallas import tpu as pltpu
from jax.sharding import PartitionSpec as P

F32, BF16 = jnp.float32, jnp.bfloat16
MESH = pl.DeviceIdType.MESH
D = 512
HEAD = 32
CELLS = 1728
WIN = 144
EPS = 1e-5
NN = (((1,), (0,)), ((), ()))
NT = (((1,), (1,)), ((), ()))
TN = (((0,), (0,)), ((), ()))
SCALE = HEAD**-0.5
SCALE_LOG2E = SCALE * math.log2(math.e)


def dot(a, b, dims=NN):
    return lax.dot_general(a, b, dims, preferred_element_type=F32)


def groups(strip):
    c = 12 * strip
    return [[(0, c, 8)], [(0, c + 8, 4), (1, c, 4)], [(1, c + 4, 8)]]


def tables():
    order = np.zeros((192, 192), np.float32)
    squeeze = np.zeros((48, 384), np.float32)
    last = np.zeros((432, 240), np.float32)
    spread = np.zeros((480, 192), np.float32)
    for c in range(8):
        for rho in range(21):
            order[(rho // 6) * 48 + c * 6 + rho % 6, c * 24 + 3 + rho] = 1
    for c in range(16):
        for r in range(3):
            squeeze[c * 3 + r, c * 24 + r] = 1
    for c in range(60):
        for r in range(3):
            spread[c * 8 + r, c * 3 + r] = 1
    for strip in range(3):
        for g, runs in enumerate(groups(strip)):
            pairs = [(lev, c + i) for lev, c, n in runs for i in range(n)]
            for p, (lev, c) in enumerate(pairs):
                at = (lev * 30 + c) * 3 if c < 30 else 192 + (lev * 6 + c - 30) * 3
                for r in range(3):
                    last[strip * 144 + g * 48 + p * 6 + 3 + r, at + r] = 1
    heads = np.zeros((128, 256), np.float32)
    for h in range(8):
        heads[16 * h : 16 * h + 16, 32 * h : 32 * h + 32] = 1
    bf = [jnp.asarray(t, BF16) for t in (order, order.T, squeeze, last, last.T, spread, heads)]
    return bf + [jnp.asarray(heads, F32)]


def slot(strip, i):
    if i == 3:
        return 9 + strip
    return strip * 3 + i


def masked_tail(x, hm):
    return jnp.concatenate([x[128:144]] * 8, 0) * hm[...]


def diagonal(ref, x, hm):
    for h in range(8):
        at = slice(128 * (h // 4), 128 * (h // 4) + 128)
        mask = jnp.concatenate([hm[16 * h : 16 * h + 16, at]] * 8, 0)
        ref[128 * h : 128 * h + 128, at] = x[:128, at] * mask
    ref[1024:1152, :] = masked_tail(x, hm)


def diagonal_t(ref, x, hm):
    turned = x[:128].T
    for h in range(8):
        ref[32 * h : 32 * h + 32, 128 * h : 128 * h + 128] = turned[32 * h : 32 * h + 32]
    ref[:, 1024:1152] = masked_tail(x, hm).T


def by_query(dst, src):
    for h in range(8):
        at = slice(128 * h, 128 * h + 128)
        dst[:, at] = src[0:128, at].T
    ends = [src[128:144, 128 * h : 128 * h + 128] for h in range(8)]
    dst[:, 1024:1152] = jnp.concatenate(ends, 0).T


def last_queries(src, x, hmf):
    each = dot(src[:, 1024:1152], x, TN) * hmf[...]
    return each.reshape(8, 16, 256).sum(0)


def attend(w, lo, proj, datt, bias, hm, hmf, att, dproj, bufs):
    qt, dt, sc, dw, pt, gt, pq, gq, qd, dd, kd, vd = bufs
    rows = pl.ds(pl.multiple_of(w * WIN, 16), WIN)
    cols = lambda off: pl.ds(pl.multiple_of(off + lo, 256), 256)
    q, k, v = proj[rows, cols(0)], proj[rows, cols(512)], proj[rows, cols(1024)]
    da = datt[rows, cols(0)]
    diagonal_t(qt, q, hm)
    diagonal_t(dt, da, hm)
    sc[...] = dot(k, qt[...])
    dw[...] = dot(v, dt[...])
    for c in range(9):
        at = slice(128 * c, 128 * c + 128)
        s = sc[:, at] + (bias[:, :128] if c < 8 else bias[:, 128:256])
        d = dw[:, at]
        e = jnp.exp2((s - jnp.max(s, 0, keepdims=True)) * SCALE_LOG2E)
        p = e * (1.0 / jnp.sum(e, 0, keepdims=True))
        pt[:, at] = p.astype(BF16)
        gt[:, at] = (p * (d - jnp.sum(p * d, 0, keepdims=True)) * SCALE).astype(BF16)
    diagonal(dd, da, hm)
    dproj[rows, cols(1024)] = dot(pt[...], dd[...]).astype(BF16)
    by_query(pq, pt)
    diagonal(vd, v, hm)
    a = jnp.concatenate([dot(pq[...], vd[...]), last_queries(pt, v, hmf)], 0)
    att[rows, cols(0)] = a.astype(BF16)
    diagonal(qd, q, hm)
    dproj[rows, cols(512)] = dot(gt[...], qd[...]).astype(BF16)
    by_query(gq, gt)
    diagonal(kd, k, hm)
    dq = jnp.concatenate([dot(gq[...], kd[...]), last_queries(gt, k, hmf)], 0)
    dproj[rows, cols(0)] = dq.astype(BF16)


def kernel(
    tok, cot, gain, wqkv, wo, order, place, squeeze, late, late_t, hm, hmf,
    by_window, lonin, latin, dqkv, dwo,
    own, edge, halo, lsend, region, lout,
    tw, cw, hid, hidt, attt, inv, mean, proj, datt, att, dproj, bias, *more,
):
    bufs, more = more[:12], more[12:]
    sums = (more[:14], more[14:28])
    local, send, recv = more[28:]
    lon, lat = lax.axis_index("lon"), lax.axis_index("lat")
    lons, lats = lax.axis_size("lon"), lax.axis_size("lat")
    z, yl, core = lon // 4, (lon // 2) % 2, lon % 2
    yh, x = lat // 4, lat % 4
    west, east = (lon + lons - 1) % lons, (lon + 1) % lons
    south, north = (lat + lats - 1) % lats, (lat + 1) % lats
    dev = lambda a, b: {"lon": a, "lat": b}
    flip = lambda bit: 1 - bit
    twin = dev(z * 4 + yl * 2 + flip(core), lat)
    zs = [(z + d) % 4 for d in (1, 2, 3)]
    xs = [(x + d) % 4 for d in (1, 2, 3)]
    ys = [(flip(yl), yh), (yl, flip(yh)), (flip(yl), flip(yh))]
    zdev = [dev(a * 4 + yl * 2 + core, lat) for a in zs]
    ydev = [dev(z * 4 + a * 2 + core, b * 4 + x) for a, b in ys]
    xdev = [dev(lon, yh * 4 + a) for a in xs]

    loads = []
    for a, ref in enumerate((tok, cot)):
        loads.append(
            pltpu.make_async_copy(ref.at[:, 144:864], own.at[a, :, 0:720], local.at[2 * a])
        )
        loads.append(pltpu.make_async_copy(ref.at[:, 0:144], edge.at[a], local.at[2 * a + 1]))
    for copy in loads:
        copy.start()
    barrier = pltpu.get_barrier_semaphore()
    halo_devs = [dev(west, lat), dev(lon, south), dev(west, south)]
    halo_devs += [dev(east, lat), dev(lon, north), dev(east, north)]
    for target in halo_devs + [twin] + zdev + ydev + xdev:
        pl.semaphore_signal(barrier, inc=1, device_id=target, device_id_type=MESH)

    used = [0]

    def remote(src, dst, target):
        n = used[0]
        used[0] += 1
        return pltpu.make_async_remote_copy(
            src_ref=src,
            dst_ref=dst,
            send_sem=send.at[n],
            recv_sem=recv.at[n],
            device_id=target,
            device_id_type=MESH,
        )

    halo_in, halo_out = [], []
    for a, ref in enumerate((tok, cot)):
        halo_in.append(remote(ref.at[:, 0:144], own.at[a, :, 720:864], dev(west, lat)))
        halo_out.append(remote(region.at[a, :, 144:288], lonin.at[a], dev(east, lat)))
    for a in range(2):
        for rows, lon_in, lon_out in ((slice(0, 192), lon, lon), (slice(192, 240), west, east)):
            halo_in.append(remote(lsend.at[a, rows], halo.at[a, rows], dev(lon_in, south)))
            halo_out.append(remote(lout.at[a, rows], latin.at[a, rows], dev(lon_out, north)))

    for n in (0, 1, 8, 9, 10, 11):
        bufs[n][...] = jnp.zeros_like(bufs[n])

    class Scatter:
        def __init__(self, refs, w):
            (self.gw, self.s0, self.r0, self.s1a, self.r1a, self.s1b, self.r1b,
             self.s2a, self.r2a, self.s2b, self.r2b, self.s3, self.r3, self.own_b) = refs
            self.left, self.right = slice(0, w), slice(w, 2 * w)
            self.cores = [
                remote(self.s0.at[:, :, c], self.r0.at[:, :, c], twin)
                for c in (self.left, self.right)
            ]
            d3 = range(3)
            self.one_a = [remote(self.s1a.at[zs[d]], self.r1a.at[d], zdev[d]) for d in d3]
            self.one_b = [remote(self.s1b.at[xs[d]], self.r1b.at[d], xdev[d]) for d in d3]
            self.two_a = [remote(self.s2a.at[xs[d]], self.r2a.at[d], xdev[d]) for d in d3]
            self.two_b = [remote(self.s2b.at[zs[d]], self.r2b.at[d], zdev[d]) for d in d3]
            self.three = [remote(self.s3.at[ys[d]], self.r3.at[d], ydev[d]) for d in d3]

        def put(self, lo, grad):
            grad_scale = 1.0 / math.sqrt(CELLS * 128)
            grad = (grad * grad_scale).reshape(8, 2, 32, 256)
            one, two = grad[:, 0], grad[:, 1]
            self.gw[:, :, lo : lo + 256] = jnp.where(core == 0, one, two)
            self.s0[:, :, lo : lo + 256] = jnp.where(core == 0, two, one).astype(BF16)

        def by_x(self, low, high):
            pick = lambda t, n: [t[4 * n : 4 * n + 4], t[16 + 4 * n : 20 + 4 * n]]
            return [jnp.concatenate(pick(low, n) + pick(high, n), 0) for n in range(4)]

        def step1(self):
            self.cores[0].wait()
            for k in range(8):
                total = self.gw[k, :, self.left] + self.r0[k, :, self.left].astype(F32)
                self.gw[k, :, self.left] = total
                self.s1a[k // 2, k % 2] = total.astype(BF16)
            for copy in self.one_a:
                copy.start()
            self.cores[1].wait()
            for k in range(4):
                total = self.gw[2 * k : 2 * k + 2, :, self.right]
                total = total + self.r0[2 * k : 2 * k + 2, :, self.right].astype(F32)
                for n, rows in enumerate(self.by_x(total[0], total[1])):
                    self.own_b[n, k] = rows
                    self.s1b[n, k] = rows.astype(BF16)
            for copy in self.one_b:
                copy.start()

        def step2(self):
            for copy in self.one_a:
                copy.wait()
            both = []
            for k in range(2):
                total = self.gw[z * 2 + k, :, self.left]
                for d in range(3):
                    total = total + self.r1a[d, k].astype(F32)
                both.append(total)
            for n, rows in enumerate(self.by_x(*both)):
                self.s2a[n] = rows
            for copy in self.two_a:
                copy.start()
            for copy in self.one_b:
                copy.wait()
            for k in range(4):
                total = self.own_b[x, k]
                for d in range(3):
                    total = total + self.r1b[d, k].astype(F32)
                self.s2b[k] = total
            for copy in self.two_b:
                copy.start()

        def step3(self):
            for copy in self.two_a + self.two_b:
                copy.wait()
            left, right = self.s2a[x], self.s2b[z]
            for d in range(3):
                left = left + self.r2a[d]
                right = right + self.r2b[d]
            for k in range(4):
                self.s3[k // 2, k % 2, 0:4, :] = left[4 * k : 4 * k + 4]
                self.s3[k // 2, k % 2, 4:8, :] = right[4 * k : 4 * k + 4]
            for copy in self.three:
                copy.start()

        def result(self):
            for copy in self.three:
                copy.wait()
            total = self.s3[yl, yh] + self.r3[0] + self.r3[1] + self.r3[2]
            return jnp.concatenate([total[0:4], total[4:8]], 1)

    early, final = Scatter(sums[0], 384), Scatter(sums[1], 640)

    def rows_of(a, strip, g):
        runs = groups(strip)[g]
        return jnp.concatenate([own[a, v, c * 24 : (c + n) * 24, :] for v, c, n in runs], 0)

    def gather(strip):
        for a in range(2):
            for g in range(3):
                got = dot(order[:144, :], rows_of(a, strip, g)).astype(BF16)
                for i in range(3):
                    at = slot(strip, i) * WIN + g * 48
                    (tw, cw)[a][at : at + 48, :] = got[i * 48 : i * 48 + 48]

    def project(first, chunks):
        @pl.loop(0, chunks)
        def _(t):
            rows = pl.ds(pl.multiple_of(first + t * 432, 16), 432)
            cells = tw[rows, :].astype(F32)
            mu = jnp.mean(cells, -1, keepdims=True)
            cells = cells - mu
            iv = lax.rsqrt(jnp.mean(cells * cells, -1, keepdims=True) + EPS)
            h = (cells * iv * gain[...]).astype(BF16)
            hid[rows, :] = h
            mean[rows, :] = mu
            inv[rows, :] = iv
            for n in range(3):
                at = slice(512 * n, 512 * n + 512)
                proj[rows, at] = dot(h, wqkv[:, at]).astype(BF16)
            datt[rows, :] = dot(cw[rows, :], wo[...], NT).astype(BF16)

    res = (hid, datt)

    def outputs(first):
        @pl.loop(0, 2)
        def _(t):
            rows = pl.ds(pl.multiple_of(first + t * 432, 16), 432)
            cells = tw[rows, :].astype(F32)
            res[0][rows, :] = (cells + dot(att[rows, :], wo[...])).astype(BF16)
            u = dot(dproj[rows, :], wqkv[...], NT) * gain[...]
            iv = inv[rows, :]
            normed = (cells - mean[rows, :]) * iv
            d = u - jnp.mean(u, -1, keepdims=True)
            d = d - normed * jnp.mean(u * normed, -1, keepdims=True)
            res[1][rows, :] = (cw[rows, :].astype(F32) + iv * d).astype(BF16)

    def windows_of(a, strip, g):
        at = [slot(strip, i) * WIN + g * 48 for i in range(4)]
        return [res[a][n : n + 48, :] for n in at]

    for copy in loads:
        copy.wait()
    for a in range(2):
        lead = [own[a, 0, 0:384, :]]
        lead += [jnp.concatenate([own[a, 0, 384:720, :], own[a, 1, 0:48, :]], 0)]
        lead += [own[a, 1, 48:432, :], own[a, 1, 432:720, :]]
        lead += [jnp.concatenate([edge[a, 0], edge[a, 1]], 0)]
        for n, cells in enumerate(lead):
            small = dot(squeeze[:, : cells.shape[0]], cells).astype(BF16)
            lsend[a, 48 * n : 48 * n + 48, :] = small
    pl.semaphore_wait(barrier, 16)
    for copy in halo_in:
        copy.start()
    gather(0)
    gather(1)
    project(0, 2)

    def receive_columns():
        for copy in halo_in[:2]:
            copy.wait()
        gather(2)
        project(864, 1)

    def receive_rows():
        for copy in halo_in[2:]:
            copy.wait()
        for a in range(2):
            base = dot(late[...], halo[a])
            for strip in range(3):
                for g in range(3):
                    at = strip * WIN + g * 48
                    got = dot(order[144:192, :], rows_of(a, strip, g)) + base[at : at + 48]
                    (tw, cw)[a][1296 + at : 1344 + at, :] = got.astype(BF16)
        project(1296, 1)

    def first_gradients():
        hidt[...] = hid[...].T
        for n in range(3):
            early.put(256 * n, dot(hidt[...], dproj[:, 512 * n : 512 * n + 256]))
            if n:
                early.cores[n - 1].start()

    stores = []
    for rows in (slice(864, 1728), slice(0, 864)):
        for a in range(2):
            n = len(stores)
            stores.append(
                pltpu.make_async_copy(res[a].at[rows], by_window.at[a, rows], local.at[n])
            )

    def return_halo():
        for a in range(2):
            lout[a] = dot(late_t[...], res[a][1296:1728, :]).astype(BF16)
            for g, runs in enumerate(groups(2)):
                cells = windows_of(a, 2, g)
                whole = dot(place[...], jnp.concatenate(cells, 0)).astype(BF16)
                at = 0
                for lev, c, n in runs:
                    to = slice((c - 24) * 24, (c - 24 + n) * 24)
                    region[a, lev, to, :] = whole[at * 24 : (at + n) * 24]
                    at += n
        for copy in halo_out:
            copy.start()
        for copy in stores[:2]:
            copy.start()

    def after_rows():
        early.step1()
        outputs(864)
        return_halo()

    @pl.loop(0, 6)
    def _(part):
        pl.when(part == 1)(receive_columns)
        pl.when(part == 3)(receive_rows)
        pl.when(part == 4)(first_gradients)
        pl.when(part == 5)(after_rows)
        inner = jnp.logical_or(part == 0, part == 5)
        second = jnp.logical_or(part == 2, part >= 4)
        lo = jnp.where(second, 256, 0)
        first = jnp.where(inner, 0, jnp.where(part < 3, 6, 9))
        count = jnp.where(inner, 6, 3)
        key_side = (lax.broadcasted_iota(jnp.int32, (WIN, 1), 0) % 6) >= 3
        lane = lax.broadcasted_iota(jnp.int32, (1, 256), 1)
        query = jnp.where(lane < 128, lane, 128 + lane % 16)
        differ = key_side != ((query % 6) >= 3)
        apart = jnp.logical_and(first == 9, lat == lats - 1)
        bias[...] = jnp.where(jnp.logical_and(apart, differ), -1e30, 0.0)

        @pl.loop(first, first + count)
        def _(w):
            attend(w, lo, proj, datt, bias, hm, hmf, att, dproj, bufs)

    early.step2()
    attt[...] = att[...].T
    for n in range(5):
        if n < 3:
            grad = dot(hidt[...], dproj[:, 512 * n + 256 : 512 * n + 512])
        else:
            grad = dot(attt[...], cw[:, 256 * n - 768 : 256 * n - 512])
        final.put(256 * n, grad)
        if n in (2, 4):
            final.cores[n // 2 - 1].start()
    early.step3()
    outputs(0)
    for copy in stores[2:]:
        copy.start()
    final.step1()
    final.step2()
    grads = early.result()
    for n in range(3):
        dqkv[:, 512 * n : 512 * n + 256] = grads[:, 256 * n : 256 * n + 256]
    final.step3()
    for copy in stores + halo_out:
        copy.wait()
    grads = final.result()
    for n in range(3):
        dqkv[:, 512 * n + 256 : 512 * n + 512] = grads[:, 256 * n : 256 * n + 256]
    dwo[...] = grads[:, 768:1280]


def settle(by_window, lonin, latin, dqkv, dwo, place, spread, out, dtok, dqkv_out, dwo_out, own, edge, sem):
    dqkv_out[...] = dqkv[...]
    dwo_out[...] = dwo[...]

    def with_first(cells, first):
        cells = cells.reshape(-1, 24, D)
        first = first.reshape(-1, 8, D)
        cells = jnp.concatenate([cells[:, 0:8] + first, cells[:, 8:24]], 1)
        return cells.reshape(-1, D).astype(BF16)

    stores = []
    for a, ref in enumerate((out, dtok)):
        rows = dot(spread[:96, :48], latin[a, 192:240, :])
        for level in range(2):
            cells = lonin[a, level].astype(F32)
            edge[a, level] = with_first(cells, rows[48 * level : 48 * level + 48])
        stores.append(pltpu.make_async_copy(edge.at[a], ref.at[:, 0:144], sem.at[2 * a]))
        stores[-1].start()
        rows = dot(spread[...], latin[a, 0:192, :])
        for strip in range(3):
            for g, runs in enumerate(groups(strip)):
                at = [slot(strip, i) * WIN + g * 48 for i in range(4)]
                cells = jnp.concatenate([by_window[a, n : n + 48, :] for n in at], 0)
                whole = dot(place[...], cells)
                at = 0
                for lev, c, n in runs:
                    keep = min(n, max(0, 30 - c))
                    if keep:
                        top = (lev * 30 + c) * 8
                        part = with_first(
                            whole[at * 24 : (at + keep) * 24], rows[top : top + 8 * keep]
                        )
                        own[a, lev, c * 24 : (c + keep) * 24, :] = part
                    at += n
        stores.append(pltpu.make_async_copy(own.at[a], ref.at[:, 144:864], sem.at[2 * a + 1]))
        stores[-1].start()
    for copy in stores:
        copy.wait()


def per_device(tokens, gain, qkv_weight, out_weight, cotangent):
    by_column = lambda a: a.transpose(0, 2, 1, 3).reshape(2, 864, D)
    vmem = pl.BlockSpec(memory_space=pltpu.VMEM)
    hbm = pl.BlockSpec(memory_space=pl.ANY)
    shape = jax.ShapeDtypeStruct
    buf = lambda *dims: pltpu.VMEM(dims, BF16)
    buf32 = lambda *dims: pltpu.VMEM(dims, F32)
    order, place, squeeze, last, last_t, spread, heads, heads32 = tables()
    copies = 12 + 2 * (2 + 6 + 6 + 3)

    def scatter(w):
        return [
            buf32(8, 32, 2 * w),
            buf(8, 32, 2 * w),
            buf(8, 32, 2 * w),
            buf(4, 2, 32, w),
            buf(3, 2, 32, w),
            buf(4, 4, 16, w),
            buf(3, 4, 16, w),
            buf32(4, 16, w),
            buf32(3, 16, w),
            buf32(4, 16, w),
            buf32(3, 16, w),
            buf32(2, 2, 8, w),
            buf32(3, 8, w),
            buf32(4, 4, 16, w),
        ]

    limit = 60 * 2**20
    parts = pl.pallas_call(
        kernel,
        out_shape=(
            shape((2, CELLS, D), BF16),
            shape((2, 2, 144, D), BF16),
            shape((2, 240, D), BF16),
            shape((4, 3 * D), F32),
            shape((4, D), F32),
        ),
        in_specs=[hbm, hbm] + [vmem] * 10,
        out_specs=(hbm, hbm, hbm, vmem, vmem),
        scratch_shapes=[
            buf(2, 2, 864, D),
            buf(2, 2, 144, D),
            buf(2, 240, D),
            buf(2, 240, D),
            buf(2, 2, 288, D),
            buf(2, 240, D),
            buf(CELLS, D),
            buf(CELLS, D),
            buf(CELLS, D),
            buf(D, CELLS),
            buf(D, CELLS),
            buf32(CELLS, 1),
            buf32(CELLS, 1),
            buf(CELLS, 3 * D),
            buf(CELLS, D),
            buf(CELLS, D),
            buf(CELLS, 3 * D),
            buf32(WIN, 256),
            *[buf(256, 1152)] * 2,
            *[buf32(WIN, 1152)] * 2,
            *[buf(WIN, 1152)] * 2,
            *[buf(128, 1152)] * 2,
            *[buf(1152, 256)] * 4,
            *scatter(384),
            *scatter(640),
            pltpu.SemaphoreType.DMA((4,)),
            pltpu.SemaphoreType.DMA((copies,)),
            pltpu.SemaphoreType.DMA((copies,)),
        ],
        compiler_params=pltpu.CompilerParams(
            collective_id=0, has_side_effects=True, vmem_limit_bytes=limit
        ),
        name="block",
    )(
        by_column(tokens),
        by_column(cotangent),
        gain.reshape(1, D),
        qkv_weight,
        out_weight,
        order,
        place,
        squeeze,
        last,
        last_t,
        heads,
        heads32,
    )
    out, dtok, dqkv, dwo = pl.pallas_call(
        settle,
        out_shape=(
            shape((2, 864, D), BF16),
            shape((2, 864, D), BF16),
            shape((4, 3 * D), F32),
            shape((4, D), F32),
        ),
        in_specs=[vmem] * 7,
        out_specs=(hbm, hbm, vmem, vmem),
        scratch_shapes=[
            buf(2, 2, 720, D),
            buf(2, 2, 144, D),
            pltpu.SemaphoreType.DMA((4,)),
        ],
        compiler_params=pltpu.CompilerParams(vmem_limit_bytes=limit),
        name="settle",
    )(*parts, place, spread)
    in_place = lambda a: a.reshape(2, 36, 24, D).transpose(0, 2, 1, 3)
    return in_place(out), in_place(dtok), dqkv, dwo


def solution(mesh):
    in_specs = (P(None, "lat", "lon", None), P(), P(), P(), P(None, "lat", "lon", None))
    out_specs = (
        P(None, "lat", "lon", None),
        P(None, "lat", "lon", None),
        P(("lon", "lat"), None),
        P(("lon", "lat"), None),
    )
    return jax.shard_map(
        per_device, mesh=mesh, in_specs=in_specs, out_specs=out_specs, check_vma=False
    )
```

```python
import functools
import math

import jax
import jax.numpy as jnp
import numpy as np
from jax import lax
from jax.experimental import pallas as pl
from jax.experimental.pallas import tpu as pltpu
from jax.sharding import PartitionSpec as P

F32, BF16 = jnp.float32, jnp.bfloat16
MESH = pl.DeviceIdType.MESH
D = 512
HEAD = 32
CELLS = 1728
WIN = 144
EPS = 1e-5
NN = (((1,), (0,)), ((), ()))
NT = (((1,), (1,)), ((), ()))
TN = (((0,), (0,)), ((), ()))
SCALE = HEAD**-0.5
SCALE_LOG2E = SCALE * math.log2(math.e)


def dot(a, b, dims=NN):
    return lax.dot_general(a, b, dims, preferred_element_type=F32)


def groups(strip):
    c = 12 * strip
    return [[(0, c, 8)], [(0, c + 8, 4), (1, c, 4)], [(1, c + 4, 8)]]


def tables():
    order = np.zeros((192, 192), np.float32)
    squeeze = np.zeros((48, 384), np.float32)
    last = np.zeros((432, 240), np.float32)
    spread = np.zeros((480, 192), np.float32)
    for c in range(8):
        for rho in range(21):
            order[(rho // 6) * 48 + c * 6 + rho % 6, c * 24 + 3 + rho] = 1
    for c in range(16):
        for r in range(3):
            squeeze[c * 3 + r, c * 24 + r] = 1
    for c in range(60):
        for r in range(3):
            spread[c * 8 + r, c * 3 + r] = 1
    for strip in range(3):
        for g, runs in enumerate(groups(strip)):
            pairs = [(lev, c + i) for lev, c, n in runs for i in range(n)]
            for p, (lev, c) in enumerate(pairs):
                at = (lev * 30 + c) * 3 if c < 30 else 192 + (lev * 6 + c - 30) * 3
                for r in range(3):
                    last[strip * 144 + g * 48 + p * 6 + 3 + r, at + r] = 1
    heads = np.zeros((128, 256), np.float32)
    for h in range(8):
        heads[16 * h : 16 * h + 16, 32 * h : 32 * h + 32] = 1
    bf = [jnp.asarray(t, BF16) for t in (order, order.T, squeeze, last, last.T, spread, heads)]
    return bf + [jnp.asarray(heads, F32)]


def slot(strip, i):
    if i == 3:
        return 9 + strip
    return strip * 3 + i


def masked_tail(x, hm):
    return jnp.concatenate([x[128:144]] * 8, 0) * hm[...]


def diagonal(ref, x, hm):
    for h in range(8):
        at = slice(128 * (h // 4), 128 * (h // 4) + 128)
        mask = jnp.concatenate([hm[16 * h : 16 * h + 16, at]] * 8, 0)
        ref[128 * h : 128 * h + 128, at] = x[:128, at] * mask
    ref[1024:1152, :] = masked_tail(x, hm)


def diagonal_t(ref, x, hm):
    turned = x[:128].T
    for h in range(8):
        ref[32 * h : 32 * h + 32, 128 * h : 128 * h + 128] = turned[32 * h : 32 * h + 32]
    ref[:, 1024:1152] = masked_tail(x, hm).T


def by_query(dst, src):
    for h in range(8):
        at = slice(128 * h, 128 * h + 128)
        dst[:, at] = src[0:128, at].T
    ends = [src[128:144, 128 * h : 128 * h + 128] for h in range(8)]
    dst[:, 1024:1152] = jnp.concatenate(ends, 0).T


def last_queries(src, x, hmf):
    each = dot(src[:, 1024:1152], x, TN) * hmf[...]
    return each.reshape(8, 16, 256).sum(0)


def attend(w, lo, proj, datt, bias, hm, hmf, att, dproj, bufs):
    qt, dt, sc, dw, pt, gt, pq, gq, qd, dd, kd, vd = bufs
    rows = pl.ds(pl.multiple_of(w * WIN, 16), WIN)
    cols = lambda off: pl.ds(pl.multiple_of(off + lo, 256), 256)
    q, k, v = proj[rows, cols(0)], proj[rows, cols(512)], proj[rows, cols(1024)]
    da = datt[rows, cols(0)]
    diagonal_t(qt, q, hm)
    diagonal_t(dt, da, hm)
    sc[...] = dot(k, qt[...])
    dw[...] = dot(v, dt[...])
    for c in range(9):
        at = slice(128 * c, 128 * c + 128)
        s = sc[:, at] + (bias[:, :128] if c < 8 else bias[:, 128:256])
        d = dw[:, at]
        e = jnp.exp2((s - jnp.max(s, 0, keepdims=True)) * SCALE_LOG2E)
        p = e * (1.0 / jnp.sum(e, 0, keepdims=True))
        pt[:, at] = p.astype(BF16)
        gt[:, at] = (p * (d - jnp.sum(p * d, 0, keepdims=True)) * SCALE).astype(BF16)
    diagonal(dd, da, hm)
    dproj[rows, cols(1024)] = dot(pt[...], dd[...]).astype(BF16)
    by_query(pq, pt)
    diagonal(vd, v, hm)
    a = jnp.concatenate([dot(pq[...], vd[...]), last_queries(pt, v, hmf)], 0)
    att[rows, cols(0)] = a.astype(BF16)
    diagonal(qd, q, hm)
    dproj[rows, cols(512)] = dot(gt[...], qd[...]).astype(BF16)
    by_query(gq, gt)
    diagonal(kd, k, hm)
    dq = jnp.concatenate([dot(gq[...], kd[...]), last_queries(gt, k, hmf)], 0)
    dproj[rows, cols(0)] = dq.astype(BF16)


def kernel(
    tok, cot, gain, wqkv, wo, order, place, squeeze, late, late_t, spread, hm, hmf,
    out, dtok, dqkv, dwo,
    own, edge, halo, lsend, region, lout, lonin, latin,
    tw, cw, hid, hidt, attt, inv, mean, proj, datt, att, dproj, bias, *more,
):
    bufs, more = more[:12], more[12:]
    sums = (more[:16], more[16:32])
    local, send, recv = more[32:]
    lon, lat = lax.axis_index("lon"), lax.axis_index("lat")
    lons, lats = lax.axis_size("lon"), lax.axis_size("lat")
    z, yl, core = lon // 4, (lon // 2) % 2, lon % 2
    yh, x = lat // 4, lat % 4
    west, east = (lon + lons - 1) % lons, (lon + 1) % lons
    south, north = (lat + lats - 1) % lats, (lat + 1) % lats
    dev = lambda a, b: {"lon": a, "lat": b}
    flip = lambda bit: 1 - bit
    twin = dev(z * 4 + yl * 2 + flip(core), lat)
    zs = [(z + d) % 4 for d in (1, 2, 3)]
    xs = [(x + d) % 4 for d in (1, 2, 3)]
    ys = [(flip(yl), yh), (yl, flip(yh)), (flip(yl), flip(yh))]
    zdev = [dev(a * 4 + yl * 2 + core, lat) for a in zs]
    ydev = [dev(z * 4 + a * 2 + core, b * 4 + x) for a, b in ys]
    xdev = [dev(lon, yh * 4 + a) for a in xs]

    loads = []
    for a, ref in enumerate((tok, cot)):
        loads.append(
            pltpu.make_async_copy(ref.at[:, 144:864], own.at[a, :, 0:720], local.at[2 * a])
        )
        loads.append(pltpu.make_async_copy(ref.at[:, 0:144], edge.at[a], local.at[2 * a + 1]))
    for copy in loads:
        copy.start()
    barrier = pltpu.get_barrier_semaphore()
    halo_devs = [dev(west, lat), dev(lon, south), dev(west, south)]
    halo_devs += [dev(east, lat), dev(lon, north), dev(east, north)]
    for target in halo_devs + [twin] + zdev + ydev + xdev:
        pl.semaphore_signal(barrier, inc=1, device_id=target, device_id_type=MESH)

    used = [0]

    def remote(src, dst, target):
        n = used[0]
        used[0] += 1
        return pltpu.make_async_remote_copy(
            src_ref=src,
            dst_ref=dst,
            send_sem=send.at[n],
            recv_sem=recv.at[n],
            device_id=target,
            device_id_type=MESH,
        )

    halo_in, halo_out = [], []
    for a in range(2):
        halo_in.append(remote(edge.at[a], own.at[a, :, 720:864], dev(west, lat)))
        halo_out.append(remote(region.at[a, :, 144:288], lonin.at[a], dev(east, lat)))
    for a in range(2):
        for rows, lon_in, lon_out in ((slice(0, 192), lon, lon), (slice(192, 240), west, east)):
            halo_in.append(remote(lsend.at[a, rows], halo.at[a, rows], dev(lon_in, south)))
            halo_out.append(remote(lout.at[a, rows], latin.at[a, rows], dev(lon_out, north)))

    for n in (0, 1, 8, 9, 10, 11):
        bufs[n][...] = jnp.zeros_like(bufs[n])

    class Scatter:
        def __init__(self, refs, w):
            (self.gw, self.s0, self.r0, self.s1a, self.r1a, self.s1b, self.r1b,
             self.s2a, self.r2a, self.s2b, self.r2b, self.s3, self.r3,
             self.own_b, self.own_a, self.own_c) = refs
            self.left, self.right = slice(0, w), slice(w, 2 * w)
            self.cores = [
                remote(self.s0.at[:, :, c], self.r0.at[:, :, c], twin)
                for c in (self.left, self.right)
            ]
            d3 = range(3)
            self.one_a = [remote(self.s1a.at[zs[d]], self.r1a.at[d], zdev[d]) for d in d3]
            self.one_b = [remote(self.s1b.at[xs[d]], self.r1b.at[d], xdev[d]) for d in d3]
            self.two_a = [remote(self.s2a.at[xs[d]], self.r2a.at[d], xdev[d]) for d in d3]
            self.two_b = [remote(self.s2b.at[zs[d]], self.r2b.at[d], zdev[d]) for d in d3]
            self.three = [remote(self.s3.at[ys[d]], self.r3.at[d], ydev[d]) for d in d3]

        def put(self, lo, grad):
            grad_scale = 1.0 / math.sqrt(CELLS * 128)
            grad = (grad * grad_scale).reshape(8, 2, 32, 256)
            one, two = grad[:, 0], grad[:, 1]
            self.gw[:, :, lo : lo + 256] = jnp.where(core == 0, one, two)
            self.s0[:, :, lo : lo + 256] = jnp.where(core == 0, two, one).astype(BF16)

        def by_x(self, low, high):
            pick = lambda t, n: [t[4 * n : 4 * n + 4], t[16 + 4 * n : 20 + 4 * n]]
            return [jnp.concatenate(pick(low, n) + pick(high, n), 0) for n in range(4)]

        def step1a(self):
            self.cores[0].wait()
            for k in range(8):
                total = self.gw[k, :, self.left] + self.r0[k, :, self.left].astype(F32)
                self.gw[k, :, self.left] = total
                self.s1a[k // 2, k % 2] = total.astype(BF16)
            for copy in self.one_a:
                copy.start()

        def step1b(self):
            self.cores[1].wait()
            for k in range(4):
                total = self.gw[2 * k : 2 * k + 2, :, self.right]
                total = total + self.r0[2 * k : 2 * k + 2, :, self.right].astype(F32)
                for n, rows in enumerate(self.by_x(total[0], total[1])):
                    self.own_b[n, k] = rows
                    self.s1b[n, k] = rows.astype(BF16)
            for copy in self.one_b:
                copy.start()

        def step2(self):
            for copy in self.one_a:
                copy.wait()
            both = []
            for k in range(2):
                total = self.gw[z * 2 + k, :, self.left]
                for d in range(3):
                    total = total + self.r1a[d, k].astype(F32)
                both.append(total)
            for n, rows in enumerate(self.by_x(*both)):
                self.own_a[n] = rows
                self.s2a[n] = rows.astype(BF16)
            for copy in self.two_a:
                copy.start()
            for copy in self.one_b:
                copy.wait()
            for k in range(4):
                total = self.own_b[x, k]
                for d in range(3):
                    total = total + self.r1b[d, k].astype(F32)
                self.own_c[k] = total
                self.s2b[k] = total.astype(BF16)
            for copy in self.two_b:
                copy.start()

        def step3(self):
            for copy in self.two_a + self.two_b:
                copy.wait()
            left, right = self.own_a[x], self.own_c[z]
            for d in range(3):
                left = left + self.r2a[d].astype(F32)
                right = right + self.r2b[d].astype(F32)
            for k in range(4):
                self.s3[k // 2, k % 2, 0:4, :] = left[4 * k : 4 * k + 4]
                self.s3[k // 2, k % 2, 4:8, :] = right[4 * k : 4 * k + 4]
            for copy in self.three:
                copy.start()

        def result(self):
            for copy in self.three:
                copy.wait()
            total = self.s3[yl, yh] + self.r3[0] + self.r3[1] + self.r3[2]
            return jnp.concatenate([total[0:4], total[4:8]], 1)

    early, final = Scatter(sums[0], 384), Scatter(sums[1], 640)

    def rows_of(a, strip, g):
        runs = groups(strip)[g]
        return jnp.concatenate([own[a, v, c * 24 : (c + n) * 24, :] for v, c, n in runs], 0)

    def gather(strip):
        for a in range(2):
            for g in range(3):
                got = dot(order[:144, :], rows_of(a, strip, g)).astype(BF16)
                for i in range(3):
                    at = slot(strip, i) * WIN + g * 48
                    (tw, cw)[a][at : at + 48, :] = got[i * 48 : i * 48 + 48]

    def project(first, chunks):
        @pl.loop(0, chunks)
        def _(t):
            rows = pl.ds(pl.multiple_of(first + t * 432, 16), 432)
            cells = tw[rows, :].astype(F32)
            mu = jnp.mean(cells, -1, keepdims=True)
            cells = cells - mu
            iv = lax.rsqrt(jnp.mean(cells * cells, -1, keepdims=True) + EPS)
            h = (cells * iv * gain[...]).astype(BF16)
            hid[rows, :] = h
            mean[rows, :] = mu
            inv[rows, :] = iv
            for n in range(3):
                at = slice(512 * n, 512 * n + 512)
                proj[rows, at] = dot(h, wqkv[:, at]).astype(BF16)
            datt[rows, :] = dot(cw[rows, :], wo[...], NT).astype(BF16)

    res = (hid, datt)

    def outputs(first, chunks):
        @pl.loop(0, chunks)
        def _(t):
            rows = pl.ds(pl.multiple_of(first + t * 432, 16), 432)
            cells = tw[rows, :].astype(F32)
            res[0][rows, :] = (cells + dot(att[rows, :], wo[...])).astype(BF16)
            u = dot(dproj[rows, :], wqkv[...], NT) * gain[...]
            iv = inv[rows, :]
            normed = (cells - mean[rows, :]) * iv
            d = u - jnp.mean(u, -1, keepdims=True)
            d = d - normed * jnp.mean(u * normed, -1, keepdims=True)
            res[1][rows, :] = (cw[rows, :].astype(F32) + iv * d).astype(BF16)

    def windows_of(a, strip, g):
        at = [slot(strip, i) * WIN + g * 48 for i in range(4)]
        return [res[a][n : n + 48, :] for n in at]

    for copy in loads:
        copy.wait()
    for a in range(2):
        lead = [own[a, 0, 0:384, :]]
        lead += [jnp.concatenate([own[a, 0, 384:720, :], own[a, 1, 0:48, :]], 0)]
        lead += [own[a, 1, 48:432, :], own[a, 1, 432:720, :]]
        lead += [jnp.concatenate([edge[a, 0], edge[a, 1]], 0)]
        for n, cells in enumerate(lead):
            small = dot(squeeze[:, : cells.shape[0]], cells).astype(BF16)
            lsend[a, 48 * n : 48 * n + 48, :] = small
    pl.semaphore_wait(barrier, 16)
    for copy in halo_in:
        copy.start()
    gather(0)
    gather(1)
    project(0, 2)

    def receive_columns():
        for copy in halo_in[:2]:
            copy.wait()
        gather(2)
        project(864, 1)

    def receive_rows():
        for copy in halo_in[2:]:
            copy.wait()
        for a in range(2):
            base = dot(late[...], halo[a])
            for strip in range(3):
                for g in range(3):
                    at = strip * WIN + g * 48
                    got = dot(order[144:192, :], rows_of(a, strip, g)) + base[at : at + 48]
                    (tw, cw)[a][1296 + at : 1344 + at, :] = got.astype(BF16)
        project(1296, 1)

    def first_gradients():
        hidt[...] = hid[...].T
        for n in range(3):
            early.put(256 * n, dot(hidt[...], dproj[:, 512 * n : 512 * n + 256]))
            if n:
                early.cores[n - 1].start()

    def return_halo():
        for a in range(2):
            lout[a] = dot(late_t[...], res[a][1296:1728, :]).astype(BF16)
            for g, runs in enumerate(groups(2)):
                cells = windows_of(a, 2, g)
                whole = dot(place[...], jnp.concatenate(cells, 0)).astype(BF16)
                at = 0
                for lev, c, n in runs:
                    to = slice((c - 24) * 24, (c - 24 + n) * 24)
                    region[a, lev, to, :] = whole[at * 24 : (at + n) * 24]
                    at += n
        for copy in halo_out:
            copy.start()
    def after_rows():
        early.step1a()
        early.step1b()
        outputs(864, 2)
        return_halo()

    @pl.loop(0, 7)
    def _(part):
        pl.when(part == 2)(receive_columns)
        pl.when(part == 4)(receive_rows)
        pl.when(part == 5)(first_gradients)
        pl.when(part == 6)(after_rows)
        pick = lambda values: sum(jnp.where(part == n, v, 0) for n, v in enumerate(values) if v)
        lo = pick((0, 256, 0, 256, 0, 256, 256))
        first = pick((0, 0, 6, 6, 9, 9, 4))
        count = pick((6, 4, 3, 3, 3, 3, 2))
        key_side = (lax.broadcasted_iota(jnp.int32, (WIN, 1), 0) % 6) >= 3
        lane = lax.broadcasted_iota(jnp.int32, (1, 256), 1)
        query = jnp.where(lane < 128, lane, 128 + lane % 16)
        differ = key_side != ((query % 6) >= 3)
        apart = jnp.logical_and(first == 9, lat == lats - 1)
        bias[...] = jnp.where(jnp.logical_and(apart, differ), -1e30, 0.0)

        @pl.loop(first, first + count)
        def _(w):
            attend(w, lo, proj, datt, bias, hm, hmf, att, dproj, bufs)

    attt[...] = att[...].T
    for n in range(5):
        if n < 3:
            grad = dot(hidt[...], dproj[:, 512 * n + 256 : 512 * n + 512])
        else:
            grad = dot(attt[...], cw[:, 256 * n - 768 : 256 * n - 512])
        final.put(256 * n, grad)
        if n in (2, 4):
            final.cores[n // 2 - 1].start()
    early.step2()
    final.step1a()
    outputs(0, 1)
    final.step1b()
    early.step3()
    outputs(432, 1)
    final.step2()
    grads = early.result()
    for n in range(3):
        dqkv[:, 512 * n : 512 * n + 256] = grads[:, 256 * n : 256 * n + 256]
    final.step3()

    for copy in halo_out:
        copy.wait()

    def with_first(cells, first):
        cells = cells.reshape(-1, 24, D)
        first = first.reshape(-1, 8, D)
        cells = jnp.concatenate([cells[:, 0:8] + first, cells[:, 8:24]], 1)
        return cells.reshape(-1, D).astype(BF16)

    for a, settled in enumerate((out, dtok)):
        rows = dot(spread[:96, :48], latin[a, 192:240, :])
        for level in range(2):
            cells = lonin[a, level].astype(F32)
            settled[level, 0:144, :] = with_first(cells, rows[48 * level : 48 * level + 48])
        rows = dot(spread[...], latin[a, 0:192, :])
        for strip in range(3):
            for g, runs in enumerate(groups(strip)):
                cells = windows_of(a, strip, g)
                whole = dot(place[...], jnp.concatenate(cells, 0))
                at = 0
                for lev, c, n in runs:
                    keep = min(n, max(0, 30 - c))
                    if keep:
                        top = (lev * 30 + c) * 8
                        part = with_first(
                            whole[at * 24 : (at + keep) * 24], rows[top : top + 8 * keep]
                        )
                        settled[lev, 144 + c * 24 : 144 + (c + keep) * 24, :] = part
                    at += n

    grads = final.result()
    for n in range(3):
        dqkv[:, 512 * n + 256 : 512 * n + 512] = grads[:, 256 * n : 256 * n + 256]
    dwo[...] = grads[:, 768:1280]


def per_device(tokens, gain, qkv_weight, out_weight, cotangent):
    by_column = lambda a: a.transpose(0, 2, 1, 3).reshape(2, 864, D)
    vmem = pl.BlockSpec(memory_space=pltpu.VMEM)
    hbm = pl.BlockSpec(memory_space=pl.ANY)
    buf = lambda *dims: pltpu.VMEM(dims, BF16)
    buf32 = lambda *dims: pltpu.VMEM(dims, F32)
    order, place, squeeze, last, last_t, spread, heads, heads32 = tables()
    copies = 12 + 2 * (2 + 6 + 6 + 3)

    def scatter(w):
        return [
            buf32(8, 32, 2 * w),
            buf(8, 32, 2 * w),
            buf(8, 32, 2 * w),
            buf(4, 2, 32, w),
            buf(3, 2, 32, w),
            buf(4, 4, 16, w),
            buf(3, 4, 16, w),
            buf(4, 16, w),
            buf(3, 16, w),
            buf(4, 16, w),
            buf(3, 16, w),
            buf32(2, 2, 8, w),
            buf32(3, 8, w),
            buf32(4, 4, 16, w),
            buf32(4, 16, w),
            buf32(4, 16, w),
        ]

    limit = 60 * 2**20
    out, dtok, dqkv, dwo = pl.pallas_call(
        kernel,
        out_shape=(
            pltpu.VMEM((2, 864, D), BF16),
            pltpu.VMEM((2, 864, D), BF16),
            pltpu.VMEM((4, 3 * D), F32),
            pltpu.VMEM((4, D), F32),
        ),
        in_specs=[hbm, hbm] + [vmem] * 11,
        out_specs=(vmem,) * 4,
        scratch_shapes=[
            buf(2, 2, 864, D),
            buf(2, 2, 144, D),
            buf(2, 240, D),
            buf(2, 240, D),
            buf(2, 2, 288, D),
            buf(2, 240, D),
            buf(2, 2, 144, D),
            buf(2, 240, D),
            buf(CELLS, D),
            buf(CELLS, D),
            buf(CELLS, D),
            buf(D, CELLS),
            buf(D, CELLS),
            buf32(CELLS, 1),
            buf32(CELLS, 1),
            buf(CELLS, 3 * D),
            buf(CELLS, D),
            buf(CELLS, D),
            buf(CELLS, 3 * D),
            buf32(WIN, 256),
            *[buf(256, 1152)] * 2,
            *[buf32(WIN, 1152)] * 2,
            *[buf(WIN, 1152)] * 2,
            *[buf(128, 1152)] * 2,
            *[buf(1152, 256)] * 4,
            *scatter(384),
            *scatter(640),
            pltpu.SemaphoreType.DMA((4,)),
            pltpu.SemaphoreType.DMA((copies,)),
            pltpu.SemaphoreType.DMA((copies,)),
        ],
        compiler_params=pltpu.CompilerParams(
            collective_id=0, has_side_effects=True, vmem_limit_bytes=limit
        ),
        name="block",
    )(
        by_column(tokens),
        by_column(cotangent),
        gain.reshape(1, D),
        qkv_weight,
        out_weight,
        order,
        place,
        squeeze,
        last,
        last_t,
        spread,
        heads,
        heads32,
    )
    in_place = lambda a: a.reshape(2, 36, 24, D).transpose(0, 2, 1, 3)
    return in_place(out), in_place(dtok), dqkv, dwo


def solution(mesh):
    in_specs = (P(None, "lat", "lon", None), P(), P(), P(), P(None, "lat", "lon", None))
    out_specs = (
        P(None, "lat", "lon", None),
        P(None, "lat", "lon", None),
        P(("lon", "lat"), None),
        P(("lon", "lat"), None),
    )
    return jax.shard_map(
        per_device, mesh=mesh, in_specs=in_specs, out_specs=out_specs, check_vma=False
    )
```

```python
import functools
import math

import jax
import jax.numpy as jnp
import numpy as np
from jax import lax
from jax.experimental import pallas as pl
from jax.experimental.pallas import tpu as pltpu
from jax.sharding import PartitionSpec as P

F32, BF16 = jnp.float32, jnp.bfloat16
MESH = pl.DeviceIdType.MESH
D = 512
HEAD = 32
CELLS = 1728
WIN = 144
EPS = 1e-5
NN = (((1,), (0,)), ((), ()))
NT = (((1,), (1,)), ((), ()))
TN = (((0,), (0,)), ((), ()))
SCALE = HEAD**-0.5
SCALE_LOG2E = SCALE * math.log2(math.e)


def dot(a, b, dims=NN):
    return lax.dot_general(a, b, dims, preferred_element_type=F32)


def groups(strip):
    c = 12 * strip
    return [[(0, c, 8)], [(0, c + 8, 4), (1, c, 4)], [(1, c + 4, 8)]]


def tables():
    order = np.zeros((192, 192), np.float32)
    squeeze = np.zeros((48, 384), np.float32)
    last = np.zeros((432, 240), np.float32)
    spread = np.zeros((480, 192), np.float32)
    for c in range(8):
        for rho in range(21):
            order[(rho // 6) * 48 + c * 6 + rho % 6, c * 24 + 3 + rho] = 1
    for c in range(16):
        for r in range(3):
            squeeze[c * 3 + r, c * 24 + r] = 1
    for c in range(60):
        for r in range(3):
            spread[c * 8 + r, c * 3 + r] = 1
    for strip in range(3):
        for g, runs in enumerate(groups(strip)):
            pairs = [(lev, c + i) for lev, c, n in runs for i in range(n)]
            for p, (lev, c) in enumerate(pairs):
                at = (lev * 30 + c) * 3 if c < 30 else 192 + (lev * 6 + c - 30) * 3
                for r in range(3):
                    last[strip * 144 + g * 48 + p * 6 + 3 + r, at + r] = 1
    heads = np.zeros((128, 256), np.float32)
    for h in range(8):
        heads[16 * h : 16 * h + 16, 32 * h : 32 * h + 32] = 1
    bf = [jnp.asarray(t, BF16) for t in (order, order.T, squeeze, last, last.T, spread, heads)]
    return bf + [jnp.asarray(heads, F32)]


def slot(strip, i):
    if i == 3:
        return 9 + strip
    return strip * 3 + i


def masked_tail(x, hm):
    return jnp.concatenate([x[128:144]] * 8, 0) * hm[...]


def diagonal(ref, x, hm):
    for h in range(8):
        at = slice(128 * (h // 4), 128 * (h // 4) + 128)
        mask = jnp.concatenate([hm[16 * h : 16 * h + 16, at]] * 8, 0)
        ref[128 * h : 128 * h + 128, at] = x[:128, at] * mask
    ref[1024:1152, :] = masked_tail(x, hm)


def by_query(dst, src):
    for h in range(8):
        at = slice(128 * h, 128 * h + 128)
        dst[:, at] = src[0:128, at].T
    ends = [src[128:144, 128 * h : 128 * h + 128] for h in range(8)]
    dst[:, 1024:1152] = jnp.concatenate(ends, 0).T


def last_queries(src, x, hmf):
    each = dot(src[:, 1024:1152], x, TN) * hmf[...]
    return each.reshape(8, 16, 256).sum(0)


def attend(w, lo, proj, datt, bias, hm, hmf, att, dproj, bufs):
    pt, gt, pq, gq, qd, dd, kd, vd = bufs
    rows = pl.ds(pl.multiple_of(w * WIN, 16), WIN)
    cols = lambda off: pl.ds(pl.multiple_of(off + lo, 256), 256)
    q, k, v = proj[rows, cols(0)], proj[rows, cols(512)], proj[rows, cols(1024)]
    da = datt[rows, cols(0)]
    diagonal(qd, q, hm)
    diagonal(dd, da, hm)
    for c in range(0, 1152, 384):
        scores = dot(k, qd[c : c + 384, :], NT)
        d_weights = dot(v, dd[c : c + 384, :], NT)
        for n in range(0, 384, 128):
            at = slice(c + n, c + n + 128)
            s = scores[:, n : n + 128] + (bias[:, :128] if c + n < 1024 else bias[:, 128:256])
            d = d_weights[:, n : n + 128]
            e = jnp.exp2((s - jnp.max(s, 0, keepdims=True)) * SCALE_LOG2E)
            p = e * (1.0 / jnp.sum(e, 0, keepdims=True))
            pt[:, at] = p.astype(BF16)
            gt[:, at] = (p * (d - jnp.sum(p * d, 0, keepdims=True)) * SCALE).astype(BF16)
    dproj[rows, cols(1024)] = dot(pt[...], dd[...]).astype(BF16)
    by_query(pq, pt)
    diagonal(vd, v, hm)
    a = jnp.concatenate([dot(pq[...], vd[...]), last_queries(pt, v, hmf)], 0)
    att[rows, cols(0)] = a.astype(BF16)
    dproj[rows, cols(512)] = dot(gt[...], qd[...]).astype(BF16)
    by_query(gq, gt)
    diagonal(kd, k, hm)
    dq = jnp.concatenate([dot(gq[...], kd[...]), last_queries(gt, k, hmf)], 0)
    dproj[rows, cols(0)] = dq.astype(BF16)


def kernel(
    tok, cot, gain, hbm_wqkv, hbm_wo, hbm_order, hbm_place, hbm_squeeze, hbm_late, hbm_late_t, hbm_spread, hbm_hm, hbm_hmf,
    out, dtok, dqkv, dwo,
    wqkv, wo, order, place, squeeze, late, late_t, spread, hm, hmf, extra,
    own, edge, halo, lsend, region, lout, lonin, latin,
    tw, cw, hid, hidt, attt, inv, mean, proj, datt, att, dproj, bias, *more,
):
    bufs, more = more[:8], more[8:]
    sums = (more[:16], more[16:32])
    local, send, recv = more[32:]
    lon, lat = lax.axis_index("lon"), lax.axis_index("lat")
    lons, lats = lax.axis_size("lon"), lax.axis_size("lat")
    z, yl, core = lon // 4, (lon // 2) % 2, lon % 2
    yh, x = lat // 4, lat % 4
    west, east = (lon + lons - 1) % lons, (lon + 1) % lons
    south, north = (lat + lats - 1) % lats, (lat + 1) % lats
    dev = lambda a, b: {"lon": a, "lat": b}
    flip = lambda bit: 1 - bit
    twin = dev(z * 4 + yl * 2 + flip(core), lat)
    zs = [(z + d) % 4 for d in (1, 2, 3)]
    xs = [(x + d) % 4 for d in (1, 2, 3)]
    ys = [(flip(yl), yh), (yl, flip(yh)), (flip(yl), flip(yh))]
    zdev = [dev(a * 4 + yl * 2 + core, lat) for a in zs]
    ydev = [dev(z * 4 + a * 2 + core, b * 4 + x) for a, b in ys]
    xdev = [dev(lon, yh * 4 + a) for a in xs]

    loads = []
    for a, ref in enumerate((tok, cot)):
        loads.append(
            pltpu.make_async_copy(ref.at[:, 144:864], own.at[a, :, 0:720], local.at[2 * a])
        )
        loads.append(pltpu.make_async_copy(ref.at[:, 0:144], edge.at[a], local.at[2 * a + 1]))
    for copy in loads:
        copy.start()
    tables_in = (hbm_squeeze, hbm_order, hbm_wqkv, hbm_wo, hbm_hm, hbm_hmf, hbm_place, hbm_late, hbm_late_t, hbm_spread)
    tables_to = (squeeze, order, wqkv, wo, hm, hmf, place, late, late_t, spread)
    params = [
        pltpu.make_async_copy(src, dst, extra.at[n])
        for n, (src, dst) in enumerate(zip(tables_in, tables_to))
    ]
    for copy in params:
        copy.start()
    barrier = pltpu.get_barrier_semaphore()
    halo_devs = [dev(west, lat), dev(lon, south), dev(west, south)]
    halo_devs += [dev(east, lat), dev(lon, north), dev(east, north)]
    for target in halo_devs + [twin] + zdev + ydev + xdev:
        pl.semaphore_signal(barrier, inc=1, device_id=target, device_id_type=MESH)

    used = [0]

    def remote(src, dst, target):
        n = used[0]
        used[0] += 1
        return pltpu.make_async_remote_copy(
            src_ref=src,
            dst_ref=dst,
            send_sem=send.at[n],
            recv_sem=recv.at[n],
            device_id=target,
            device_id_type=MESH,
        )

    halo_in, halo_out = [], []
    for a in range(2):
        halo_in.append(remote(edge.at[a], own.at[a, :, 720:864], dev(west, lat)))
        halo_out.append(remote(region.at[a, :, 144:288], lonin.at[a], dev(east, lat)))
    for a in range(2):
        for rows, lon_in, lon_out in ((slice(0, 192), lon, lon), (slice(192, 240), west, east)):
            halo_in.append(remote(lsend.at[a, rows], halo.at[a, rows], dev(lon_in, south)))
            halo_out.append(remote(lout.at[a, rows], latin.at[a, rows], dev(lon_out, north)))

    for n in (4, 5, 6, 7):
        bufs[n][...] = jnp.zeros_like(bufs[n])

    class Scatter:
        def __init__(self, refs, w):
            (self.gw, self.s0, self.r0, self.s1a, self.r1a, self.s1b, self.r1b,
             self.s2a, self.r2a, self.s2b, self.r2b, self.s3, self.r3,
             self.own_b, self.own_a, self.own_c) = refs
            self.left, self.right = slice(0, w), slice(w, 2 * w)
            self.cores = [
                remote(self.s0.at[:, :, c], self.r0.at[:, :, c], twin)
                for c in (self.left, self.right)
            ]
            d3 = range(3)
            self.one_a = [remote(self.s1a.at[zs[d]], self.r1a.at[d], zdev[d]) for d in d3]
            self.one_b = [remote(self.s1b.at[xs[d]], self.r1b.at[d], xdev[d]) for d in d3]
            self.two_a = [remote(self.s2a.at[xs[d]], self.r2a.at[d], xdev[d]) for d in d3]
            self.two_b = [remote(self.s2b.at[zs[d]], self.r2b.at[d], zdev[d]) for d in d3]
            self.three = [remote(self.s3.at[ys[d]], self.r3.at[d], ydev[d]) for d in d3]

        def put(self, lo, grad):
            grad_scale = 1.0 / math.sqrt(CELLS * 128)
            grad = (grad * grad_scale).reshape(8, 2, 32, 256)
            one, two = grad[:, 0], grad[:, 1]
            self.gw[:, :, lo : lo + 256] = jnp.where(core == 0, one, two)
            self.s0[:, :, lo : lo + 256] = jnp.where(core == 0, two, one).astype(BF16)

        def by_x(self, low, high):
            pick = lambda t, n: [t[4 * n : 4 * n + 4], t[16 + 4 * n : 20 + 4 * n]]
            return [jnp.concatenate(pick(low, n) + pick(high, n), 0) for n in range(4)]

        def step1a(self):
            self.cores[0].wait()
            for k in range(8):
                total = self.gw[k, :, self.left] + self.r0[k, :, self.left].astype(F32)
                self.gw[k, :, self.left] = total
                self.s1a[k // 2, k % 2] = total.astype(BF16)
            for copy in self.one_a:
                copy.start()

        def step1b(self):
            self.cores[1].wait()
            for k in range(4):
                total = self.gw[2 * k : 2 * k + 2, :, self.right]
                total = total + self.r0[2 * k : 2 * k + 2, :, self.right].astype(F32)
                for n, rows in enumerate(self.by_x(total[0], total[1])):
                    self.own_b[n, k] = rows
                    self.s1b[n, k] = rows.astype(BF16)
            for copy in self.one_b:
                copy.start()

        def step2(self):
            for copy in self.one_a:
                copy.wait()
            both = []
            for k in range(2):
                total = self.gw[z * 2 + k, :, self.left]
                for d in range(3):
                    total = total + self.r1a[d, k].astype(F32)
                both.append(total)
            for n, rows in enumerate(self.by_x(*both)):
                self.own_a[n] = rows
                self.s2a[n] = rows.astype(BF16)
            for copy in self.two_a:
                copy.start()
            for copy in self.one_b:
                copy.wait()
            for k in range(4):
                total = self.own_b[x, k]
                for d in range(3):
                    total = total + self.r1b[d, k].astype(F32)
                self.own_c[k] = total
                self.s2b[k] = total.astype(BF16)
            for copy in self.two_b:
                copy.start()

        def step3(self):
            for copy in self.two_a + self.two_b:
                copy.wait()
            left, right = self.own_a[x], self.own_c[z]
            for d in range(3):
                left = left + self.r2a[d].astype(F32)
                right = right + self.r2b[d].astype(F32)
            for k in range(4):
                self.s3[k // 2, k % 2, 0:4, :] = left[4 * k : 4 * k + 4]
                self.s3[k // 2, k % 2, 4:8, :] = right[4 * k : 4 * k + 4]
            for copy in self.three:
                copy.start()

        def result(self):
            for copy in self.three:
                copy.wait()
            total = self.s3[yl, yh] + self.r3[0] + self.r3[1] + self.r3[2]
            return jnp.concatenate([total[0:4], total[4:8]], 1)

    early, final = Scatter(sums[0], 384), Scatter(sums[1], 640)

    def rows_of(a, strip, g):
        runs = groups(strip)[g]
        return jnp.concatenate([own[a, v, c * 24 : (c + n) * 24, :] for v, c, n in runs], 0)

    def gather(strip):
        for a in range(2):
            for g in range(3):
                got = dot(order[:144, :], rows_of(a, strip, g)).astype(BF16)
                for i in range(3):
                    at = slot(strip, i) * WIN + g * 48
                    (tw, cw)[a][at : at + 48, :] = got[i * 48 : i * 48 + 48]

    def project(first, chunks):
        @pl.loop(0, chunks)
        def _(t):
            rows = pl.ds(pl.multiple_of(first + t * 432, 16), 432)
            cells = tw[rows, :].astype(F32)
            mu = jnp.mean(cells, -1, keepdims=True)
            cells = cells - mu
            iv = lax.rsqrt(jnp.mean(cells * cells, -1, keepdims=True) + EPS)
            h = (cells * iv * gain[...]).astype(BF16)
            hid[rows, :] = h
            mean[rows, :] = mu
            inv[rows, :] = iv
            for n in range(3):
                at = slice(512 * n, 512 * n + 512)
                proj[rows, at] = dot(h, wqkv[:, at]).astype(BF16)
            datt[rows, :] = dot(cw[rows, :], wo[...], NT).astype(BF16)

    res = (hid, datt)

    def outputs(first, chunks):
        @pl.loop(0, chunks)
        def _(t):
            rows = pl.ds(pl.multiple_of(first + t * 432, 16), 432)
            cells = tw[rows, :].astype(F32)
            res[0][rows, :] = (cells + dot(att[rows, :], wo[...])).astype(BF16)
            u = dot(dproj[rows, :], wqkv[...], NT) * gain[...]
            iv = inv[rows, :]
            normed = (cells - mean[rows, :]) * iv
            d = u - jnp.mean(u, -1, keepdims=True)
            d = d - normed * jnp.mean(u * normed, -1, keepdims=True)
            res[1][rows, :] = (cw[rows, :].astype(F32) + iv * d).astype(BF16)

    def windows_of(a, strip, g):
        at = [slot(strip, i) * WIN + g * 48 for i in range(4)]
        return [res[a][n : n + 48, :] for n in at]

    for copy in loads + params[:1]:
        copy.wait()
    for a in range(2):
        lead = [own[a, 0, 0:384, :]]
        lead += [jnp.concatenate([own[a, 0, 384:720, :], own[a, 1, 0:48, :]], 0)]
        lead += [own[a, 1, 48:432, :], own[a, 1, 432:720, :]]
        lead += [jnp.concatenate([edge[a, 0], edge[a, 1]], 0)]
        for n, cells in enumerate(lead):
            small = dot(squeeze[:, : cells.shape[0]], cells).astype(BF16)
            lsend[a, 48 * n : 48 * n + 48, :] = small
    pl.semaphore_wait(barrier, 16)
    for copy in halo_in:
        copy.start()
    for copy in params[1:]:
        copy.wait()
    gather(0)
    gather(1)
    project(0, 2)

    def receive_columns():
        for copy in halo_in[:2]:
            copy.wait()
        gather(2)
        project(864, 1)

    def receive_rows():
        for copy in halo_in[2:]:
            copy.wait()
        for a in range(2):
            base = dot(late[...], halo[a])
            for strip in range(3):
                for g in range(3):
                    at = strip * WIN + g * 48
                    got = dot(order[144:192, :], rows_of(a, strip, g)) + base[at : at + 48]
                    (tw, cw)[a][1296 + at : 1344 + at, :] = got.astype(BF16)
        project(1296, 1)

    def first_gradients():
        hidt[...] = hid[...].T
        for n in range(3):
            early.put(256 * n, dot(hidt[...], dproj[:, 512 * n : 512 * n + 256]))
            if n:
                early.cores[n - 1].start()

    def return_halo():
        for a in range(2):
            lout[a] = dot(late_t[...], res[a][1296:1728, :]).astype(BF16)
            for g, runs in enumerate(groups(2)):
                cells = windows_of(a, 2, g)
                whole = dot(place[...], jnp.concatenate(cells, 0)).astype(BF16)
                at = 0
                for lev, c, n in runs:
                    to = slice((c - 24) * 24, (c - 24 + n) * 24)
                    region[a, lev, to, :] = whole[at * 24 : (at + n) * 24]
                    at += n
        for copy in halo_out:
            copy.start()
    def after_rows():
        early.step1a()
        early.step1b()
        outputs(864, 2)
        return_halo()

    @pl.loop(0, 7)
    def _(part):
        pl.when(part == 2)(receive_columns)
        pl.when(part == 4)(receive_rows)
        pl.when(part == 5)(first_gradients)
        pl.when(part == 6)(after_rows)
        pick = lambda values: sum(jnp.where(part == n, v, 0) for n, v in enumerate(values) if v)
        lo = pick((0, 256, 0, 256, 0, 256, 256))
        first = pick((0, 0, 6, 6, 9, 9, 4))
        count = pick((6, 4, 3, 3, 3, 3, 2))
        key_side = (lax.broadcasted_iota(jnp.int32, (WIN, 1), 0) % 6) >= 3
        lane = lax.broadcasted_iota(jnp.int32, (1, 256), 1)
        query = jnp.where(lane < 128, lane, 128 + lane % 16)
        differ = key_side != ((query % 6) >= 3)
        apart = jnp.logical_and(first == 9, lat == lats - 1)
        bias[...] = jnp.where(jnp.logical_and(apart, differ), -1e30, 0.0)

        @pl.loop(first, first + count)
        def _(w):
            attend(w, lo, proj, datt, bias, hm, hmf, att, dproj, bufs)

    attt[...] = att[...].T
    for n in range(5):
        if n < 3:
            grad = dot(hidt[...], dproj[:, 512 * n + 256 : 512 * n + 512])
        else:
            grad = dot(attt[...], cw[:, 256 * n - 768 : 256 * n - 512])
        final.put(256 * n, grad)
        if n in (2, 4):
            final.cores[n // 2 - 1].start()
    early.step2()
    final.step1a()
    outputs(0, 1)
    final.step1b()
    early.step3()
    outputs(432, 1)
    final.step2()
    grads = early.result()
    for n in range(3):
        dqkv[:, 512 * n : 512 * n + 256] = grads[:, 256 * n : 256 * n + 256]
    final.step3()

    for copy in halo_out:
        copy.wait()

    def with_first(cells, first):
        cells = cells.reshape(-1, 24, D)
        first = first.reshape(-1, 8, D)
        cells = jnp.concatenate([cells[:, 0:8] + first, cells[:, 8:24]], 1)
        return cells.reshape(-1, D).astype(BF16)

    for a, settled in enumerate((out, dtok)):
        rows = dot(spread[:96, :48], latin[a, 192:240, :])
        for level in range(2):
            cells = lonin[a, level].astype(F32)
            settled[level, 0:144, :] = with_first(cells, rows[48 * level : 48 * level + 48])
        rows = dot(spread[...], latin[a, 0:192, :])
        for strip in range(3):
            for g, runs in enumerate(groups(strip)):
                cells = windows_of(a, strip, g)
                whole = dot(place[...], jnp.concatenate(cells, 0))
                at = 0
                for lev, c, n in runs:
                    keep = min(n, max(0, 30 - c))
                    if keep:
                        top = (lev * 30 + c) * 8
                        part = with_first(
                            whole[at * 24 : (at + keep) * 24], rows[top : top + 8 * keep]
                        )
                        settled[lev, 144 + c * 24 : 144 + (c + keep) * 24, :] = part
                    at += n

    grads = final.result()
    for n in range(3):
        dqkv[:, 512 * n + 256 : 512 * n + 512] = grads[:, 256 * n : 256 * n + 256]
    dwo[...] = grads[:, 768:1280]


def per_device(tokens, gain, qkv_weight, out_weight, cotangent):
    by_column = lambda a: a.transpose(0, 2, 1, 3).reshape(2, 864, D)
    vmem = pl.BlockSpec(memory_space=pltpu.VMEM)
    hbm = pl.BlockSpec(memory_space=pl.ANY)
    buf = lambda *dims: pltpu.VMEM(dims, BF16)
    buf32 = lambda *dims: pltpu.VMEM(dims, F32)
    order, place, squeeze, last, last_t, spread, heads, heads32 = tables()
    copies = 12 + 2 * (2 + 6 + 6 + 3)

    def scatter(w):
        return [
            buf32(8, 32, 2 * w),
            buf(8, 32, 2 * w),
            buf(8, 32, 2 * w),
            buf(4, 2, 32, w),
            buf(3, 2, 32, w),
            buf(4, 4, 16, w),
            buf(3, 4, 16, w),
            buf(4, 16, w),
            buf(3, 16, w),
            buf(4, 16, w),
            buf(3, 16, w),
            buf32(2, 2, 8, w),
            buf32(3, 8, w),
            buf32(4, 4, 16, w),
            buf32(4, 16, w),
            buf32(4, 16, w),
        ]

    limit = 60 * 2**20
    out, dtok, dqkv, dwo = pl.pallas_call(
        kernel,
        out_shape=(
            pltpu.VMEM((2, 864, D), BF16),
            pltpu.VMEM((2, 864, D), BF16),
            pltpu.VMEM((4, 3 * D), F32),
            pltpu.VMEM((4, D), F32),
        ),
        in_specs=[hbm, hbm, vmem] + [hbm] * 10,
        out_specs=(vmem,) * 4,
        scratch_shapes=[
            buf(D, 3 * D),
            buf(D, D),
            *[buf(*t.shape) for t in (order, place, squeeze, last, last_t, spread, heads)],
            buf32(*heads32.shape),
            pltpu.SemaphoreType.DMA((10,)),
            buf(2, 2, 864, D),
            buf(2, 2, 144, D),
            buf(2, 240, D),
            buf(2, 240, D),
            buf(2, 2, 288, D),
            buf(2, 240, D),
            buf(2, 2, 144, D),
            buf(2, 240, D),
            buf(CELLS, D),
            buf(CELLS, D),
            buf(CELLS, D),
            buf(D, CELLS),
            buf(D, CELLS),
            buf32(CELLS, 1),
            buf32(CELLS, 1),
            buf(CELLS, 3 * D),
            buf(CELLS, D),
            buf(CELLS, D),
            buf(CELLS, 3 * D),
            buf32(WIN, 256),
            *[buf(WIN, 1152)] * 2,
            *[buf(128, 1152)] * 2,
            *[buf(1152, 256)] * 4,
            *scatter(384),
            *scatter(640),
            pltpu.SemaphoreType.DMA((4,)),
            pltpu.SemaphoreType.DMA((copies,)),
            pltpu.SemaphoreType.DMA((copies,)),
        ],
        compiler_params=pltpu.CompilerParams(
            collective_id=0, has_side_effects=True, vmem_limit_bytes=limit
        ),
        name="block",
    )(
        by_column(tokens),
        by_column(cotangent),
        gain.reshape(1, D),
        qkv_weight,
        out_weight,
        order,
        place,
        squeeze,
        last,
        last_t,
        spread,
        heads,
        heads32,
    )
    in_place = lambda a: a.reshape(2, 36, 24, D).transpose(0, 2, 1, 3)
    return in_place(out), in_place(dtok), dqkv, dwo


def solution(mesh):
    in_specs = (P(None, "lat", "lon", None), P(), P(), P(), P(None, "lat", "lon", None))
    out_specs = (
        P(None, "lat", "lon", None),
        P(None, "lat", "lon", None),
        P(("lon", "lat"), None),
        P(("lon", "lat"), None),
    )
    return jax.shard_map(
        per_device, mesh=mesh, in_specs=in_specs, out_specs=out_specs, check_vma=False
    )
```

```python
import functools
import math

import jax
import jax.numpy as jnp
import numpy as np
from jax import lax
from jax.experimental import pallas as pl
from jax.experimental.pallas import tpu as pltpu
from jax.sharding import PartitionSpec as P

F32, BF16 = jnp.float32, jnp.bfloat16
MESH = pl.DeviceIdType.MESH
D = 512
HEAD = 32
CELLS = 1728
WIN = 144
EPS = 1e-5
NN = (((1,), (0,)), ((), ()))
NT = (((1,), (1,)), ((), ()))
TN = (((0,), (0,)), ((), ()))
SCALE = HEAD**-0.5
SCALE_LOG2E = SCALE * math.log2(math.e)


def dot(a, b, dims=NN):
    return lax.dot_general(a, b, dims, preferred_element_type=F32)


def groups(strip):
    c = 12 * strip
    return [[(0, c, 8)], [(0, c + 8, 4), (1, c, 4)], [(1, c + 4, 8)]]


def tables():
    order = np.zeros((192, 192), np.float32)
    squeeze = np.zeros((48, 384), np.float32)
    last = np.zeros((432, 240), np.float32)
    spread = np.zeros((480, 192), np.float32)
    for c in range(8):
        for rho in range(21):
            order[(rho // 6) * 48 + c * 6 + rho % 6, c * 24 + 3 + rho] = 1
    for c in range(16):
        for r in range(3):
            squeeze[c * 3 + r, c * 24 + r] = 1
    for c in range(60):
        for r in range(3):
            spread[c * 8 + r, c * 3 + r] = 1
    for strip in range(3):
        for g, runs in enumerate(groups(strip)):
            pairs = [(lev, c + i) for lev, c, n in runs for i in range(n)]
            for p, (lev, c) in enumerate(pairs):
                at = (lev * 30 + c) * 3 if c < 30 else 192 + (lev * 6 + c - 30) * 3
                for r in range(3):
                    last[strip * 144 + g * 48 + p * 6 + 3 + r, at + r] = 1
    heads = np.zeros((128, 256), np.float32)
    for h in range(8):
        heads[16 * h : 16 * h + 16, 32 * h : 32 * h + 32] = 1
    bf = [jnp.asarray(t, BF16) for t in (order, order.T, squeeze, last, last.T, spread, heads)]
    return bf + [jnp.asarray(heads, F32)]


def slot(strip, i):
    if i == 3:
        return 9 + strip
    return strip * 3 + i


def masked_tail(x, hm):
    return jnp.concatenate([x[128:144]] * 8, 0) * hm[...]


def diagonal(ref, x, hm):
    for h in range(8):
        at = slice(128 * (h // 4), 128 * (h // 4) + 128)
        mask = jnp.concatenate([hm[16 * h : 16 * h + 16, at]] * 8, 0)
        ref[128 * h : 128 * h + 128, at] = x[:128, at] * mask
    ref[1024:1152, :] = masked_tail(x, hm)


def by_query(dst, src):
    for h in range(8):
        at = slice(128 * h, 128 * h + 128)
        dst[:, at] = src[0:128, at].T
    ends = [src[128:144, 128 * h : 128 * h + 128] for h in range(8)]
    dst[:, 1024:1152] = jnp.concatenate(ends, 0).T


def last_queries(src, x, hmf):
    each = dot(src[:, 1024:1152], x, TN) * hmf[...]
    return each.reshape(8, 16, 256).sum(0)


def attend(w, lo, proj, datt, bias, hm, hmf, att, dproj, bufs):
    pt, gt, pq, gq, qd, dd, kd, vd = bufs
    rows = pl.ds(pl.multiple_of(w * WIN, 16), WIN)
    cols = lambda off: pl.ds(pl.multiple_of(off + lo, 256), 256)
    q, k, v = proj[rows, cols(0)], proj[rows, cols(512)], proj[rows, cols(1024)]
    da = datt[rows, cols(0)]
    diagonal(qd, q, hm)
    diagonal(dd, da, hm)
    for c in range(0, 1152, 384):
        scores = dot(k, qd[c : c + 384, :], NT)
        d_weights = dot(v, dd[c : c + 384, :], NT)
        for n in range(0, 384, 128):
            at = slice(c + n, c + n + 128)
            s = scores[:, n : n + 128] + (bias[:, :128] if c + n < 1024 else bias[:, 128:256])
            d = d_weights[:, n : n + 128]
            e = jnp.exp2((s - jnp.max(s, 0, keepdims=True)) * SCALE_LOG2E)
            p = e * (1.0 / jnp.sum(e, 0, keepdims=True))
            pt[:, at] = p.astype(BF16)
            gt[:, at] = (p * (d - jnp.sum(p * d, 0, keepdims=True)) * SCALE).astype(BF16)
    dproj[rows, cols(1024)] = dot(pt[...], dd[...]).astype(BF16)
    by_query(pq, pt)
    diagonal(vd, v, hm)
    a = jnp.concatenate([dot(pq[...], vd[...]), last_queries(pt, v, hmf)], 0)
    att[rows, cols(0)] = a.astype(BF16)
    dproj[rows, cols(512)] = dot(gt[...], qd[...]).astype(BF16)
    by_query(gq, gt)
    diagonal(kd, k, hm)
    dq = jnp.concatenate([dot(gq[...], kd[...]), last_queries(gt, k, hmf)], 0)
    dproj[rows, cols(0)] = dq.astype(BF16)


def kernel(
    tok, cot, gain, hbm_wqkv, hbm_wo, hbm_order, hbm_place, hbm_squeeze, hbm_late, hbm_late_t, hbm_spread, hbm_hm, hbm_hmf,
    out, dtok, dqkv, dwo,
    wqkv, wo, order, place, squeeze, late, late_t, spread, hm, hmf, extra,
    own, edge, halo, lsend, region, lout, lonin, latin,
    tw, cw, hid, hidt, attt, inv, mean, proj, datt, att, dproj, bias, *more,
):
    bufs, more = more[:8], more[8:]
    sums = (more[:16], more[16:32])
    local, send, recv = more[32:]
    lon, lat = lax.axis_index("lon"), lax.axis_index("lat")
    lons, lats = lax.axis_size("lon"), lax.axis_size("lat")
    z, yl, core = lon // 4, (lon // 2) % 2, lon % 2
    yh, x = lat // 4, lat % 4
    west, east = (lon + lons - 1) % lons, (lon + 1) % lons
    south, north = (lat + lats - 1) % lats, (lat + 1) % lats
    dev = lambda a, b: {"lon": a, "lat": b}
    flip = lambda bit: 1 - bit
    twin = dev(z * 4 + yl * 2 + flip(core), lat)
    zs = [(z + d) % 4 for d in (1, 2, 3)]
    xs = [(x + d) % 4 for d in (1, 2, 3)]
    ys = [(flip(yl), yh), (yl, flip(yh)), (flip(yl), flip(yh))]
    zdev = [dev(a * 4 + yl * 2 + core, lat) for a in zs]
    ydev = [dev(z * 4 + a * 2 + core, b * 4 + x) for a, b in ys]
    xdev = [dev(lon, yh * 4 + a) for a in xs]

    loads = []
    for a, ref in enumerate((tok, cot)):
        loads.append(
            pltpu.make_async_copy(ref.at[:, 144:864], own.at[a, :, 0:720], local.at[2 * a])
        )
        loads.append(pltpu.make_async_copy(ref.at[:, 0:144], edge.at[a], local.at[2 * a + 1]))
    for copy in loads:
        copy.start()
    tables_in = (hbm_squeeze, hbm_order, hbm_wqkv, hbm_wo, hbm_hm, hbm_hmf, hbm_place, hbm_late, hbm_late_t, hbm_spread)
    tables_to = (squeeze, order, wqkv, wo, hm, hmf, place, late, late_t, spread)
    params = [
        pltpu.make_async_copy(src, dst, extra.at[n])
        for n, (src, dst) in enumerate(zip(tables_in, tables_to))
    ]
    for copy in params:
        copy.start()
    barrier = pltpu.get_barrier_semaphore()
    halo_devs = [dev(west, lat), dev(lon, south), dev(west, south)]
    halo_devs += [dev(east, lat), dev(lon, north), dev(east, north)]
    for target in halo_devs + [twin] + zdev + ydev + xdev:
        pl.semaphore_signal(barrier, inc=1, device_id=target, device_id_type=MESH)

    used = [0]

    def remote(src, dst, target):
        n = used[0]
        used[0] += 1
        return pltpu.make_async_remote_copy(
            src_ref=src,
            dst_ref=dst,
            send_sem=send.at[n],
            recv_sem=recv.at[n],
            device_id=target,
            device_id_type=MESH,
        )

    halo_in, halo_out = [], []
    for a in range(2):
        halo_in.append(remote(edge.at[a], own.at[a, :, 720:864], dev(west, lat)))
        halo_out.append(remote(region.at[a, :, 144:288], lonin.at[a], dev(east, lat)))
    for a in range(2):
        for rows, lon_in, lon_out in ((slice(0, 192), lon, lon), (slice(192, 240), west, east)):
            halo_in.append(remote(lsend.at[a, rows], halo.at[a, rows], dev(lon_in, south)))
            halo_out.append(remote(lout.at[a, rows], latin.at[a, rows], dev(lon_out, north)))

    for n in (4, 5, 6, 7):
        bufs[n][...] = jnp.zeros_like(bufs[n])

    class Scatter:
        def __init__(self, refs, w):
            (self.gw, self.s0, self.r0, self.s1a, self.r1a, self.s1b, self.r1b,
             self.s2a, self.r2a, self.s2b, self.r2b, self.s3, self.r3,
             self.own_b, self.own_a, self.own_c) = refs
            self.left, self.right = slice(0, w), slice(w, 2 * w)
            self.cores = [
                remote(self.s0.at[:, :, c], self.r0.at[:, :, c], twin)
                for c in (self.left, self.right)
            ]
            d3 = range(3)
            self.one_a = [remote(self.s1a.at[zs[d]], self.r1a.at[d], zdev[d]) for d in d3]
            self.one_b = [remote(self.s1b.at[xs[d]], self.r1b.at[d], xdev[d]) for d in d3]
            self.two_a = [remote(self.s2a.at[xs[d]], self.r2a.at[d], xdev[d]) for d in d3]
            self.two_b = [remote(self.s2b.at[zs[d]], self.r2b.at[d], zdev[d]) for d in d3]
            self.three = [remote(self.s3.at[ys[d]], self.r3.at[d], ydev[d]) for d in d3]

        def put(self, lo, grad):
            grad_scale = 1.0 / math.sqrt(CELLS * 128)
            grad = (grad * grad_scale).reshape(8, 2, 32, 256)
            one, two = grad[:, 0], grad[:, 1]
            self.gw[:, :, lo : lo + 256] = jnp.where(core == 0, one, two)
            self.s0[:, :, lo : lo + 256] = jnp.where(core == 0, two, one).astype(BF16)

        def by_x(self, low, high):
            pick = lambda t, n: [t[4 * n : 4 * n + 4], t[16 + 4 * n : 20 + 4 * n]]
            return [jnp.concatenate(pick(low, n) + pick(high, n), 0) for n in range(4)]

        def step1a(self):
            self.cores[0].wait()
            for k in range(8):
                total = self.gw[k, :, self.left] + self.r0[k, :, self.left].astype(F32)
                self.gw[k, :, self.left] = total
                self.s1a[k // 2, k % 2] = total.astype(BF16)
            for copy in self.one_a:
                copy.start()

        def step1b(self):
            self.cores[1].wait()
            for k in range(4):
                total = self.gw[2 * k : 2 * k + 2, :, self.right]
                total = total + self.r0[2 * k : 2 * k + 2, :, self.right].astype(F32)
                for n, rows in enumerate(self.by_x(total[0], total[1])):
                    self.own_b[n, k] = rows
                    self.s1b[n, k] = rows.astype(BF16)
            for copy in self.one_b:
                copy.start()

        def step2(self):
            for copy in self.one_a:
                copy.wait()
            both = []
            for k in range(2):
                total = self.gw[z * 2 + k, :, self.left]
                for d in range(3):
                    total = total + self.r1a[d, k].astype(F32)
                both.append(total)
            for n, rows in enumerate(self.by_x(*both)):
                self.own_a[n] = rows
                self.s2a[n] = rows.astype(BF16)
            for copy in self.two_a:
                copy.start()
            for copy in self.one_b:
                copy.wait()
            for k in range(4):
                total = self.own_b[x, k]
                for d in range(3):
                    total = total + self.r1b[d, k].astype(F32)
                self.own_c[k] = total
                self.s2b[k] = total.astype(BF16)
            for copy in self.two_b:
                copy.start()

        def step3(self):
            for copy in self.two_a + self.two_b:
                copy.wait()
            left, right = self.own_a[x], self.own_c[z]
            for d in range(3):
                left = left + self.r2a[d].astype(F32)
                right = right + self.r2b[d].astype(F32)
            for k in range(4):
                self.s3[k // 2, k % 2, 0:4, :] = left[4 * k : 4 * k + 4]
                self.s3[k // 2, k % 2, 4:8, :] = right[4 * k : 4 * k + 4]
            for copy in self.three:
                copy.start()

        def result(self):
            for copy in self.three:
                copy.wait()
            total = self.s3[yl, yh] + self.r3[0] + self.r3[1] + self.r3[2]
            return jnp.concatenate([total[0:4], total[4:8]], 1)

    early, final = Scatter(sums[0], 384), Scatter(sums[1], 640)

    def rows_of(a, strip, g):
        runs = groups(strip)[g]
        return jnp.concatenate([own[a, v, c * 24 : (c + n) * 24, :] for v, c, n in runs], 0)

    def gather(strip):
        for a in range(2):
            for g in range(3):
                got = dot(order[:144, :], rows_of(a, strip, g)).astype(BF16)
                for i in range(3):
                    at = slot(strip, i) * WIN + g * 48
                    (tw, cw)[a][at : at + 48, :] = got[i * 48 : i * 48 + 48]

    def project(first, chunks):
        @pl.loop(0, chunks)
        def _(t):
            rows = pl.ds(pl.multiple_of(first + t * 432, 16), 432)
            cells = tw[rows, :].astype(F32)
            mu = jnp.mean(cells, -1, keepdims=True)
            cells = cells - mu
            iv = lax.rsqrt(jnp.mean(cells * cells, -1, keepdims=True) + EPS)
            h = (cells * iv * gain[...]).astype(BF16)
            hid[rows, :] = h
            mean[rows, :] = mu
            inv[rows, :] = iv
            for n in range(3):
                at = slice(512 * n, 512 * n + 512)
                proj[rows, at] = dot(h, wqkv[:, at]).astype(BF16)
            datt[rows, :] = dot(cw[rows, :], wo[...], NT).astype(BF16)

    res = (hid, datt)

    def outputs(first, chunks):
        @pl.loop(0, chunks)
        def _(t):
            rows = pl.ds(pl.multiple_of(first + t * 432, 16), 432)
            cells = tw[rows, :].astype(F32)
            res[0][rows, :] = (cells + dot(att[rows, :], wo[...])).astype(BF16)
            u = dot(dproj[rows, :], wqkv[...], NT) * gain[...]
            iv = inv[rows, :]
            normed = (cells - mean[rows, :]) * iv
            d = u - jnp.mean(u, -1, keepdims=True)
            d = d - normed * jnp.mean(u * normed, -1, keepdims=True)
            res[1][rows, :] = (cw[rows, :].astype(F32) + iv * d).astype(BF16)

    def windows_of(a, strip, g):
        at = [slot(strip, i) * WIN + g * 48 for i in range(4)]
        return [res[a][n : n + 48, :] for n in at]

    for copy in loads + params[:1]:
        copy.wait()
    for a in range(2):
        lead = [own[a, 0, 0:384, :]]
        lead += [jnp.concatenate([own[a, 0, 384:720, :], own[a, 1, 0:48, :]], 0)]
        lead += [own[a, 1, 48:432, :], own[a, 1, 432:720, :]]
        lead += [jnp.concatenate([edge[a, 0], edge[a, 1]], 0)]
        for n, cells in enumerate(lead):
            small = dot(squeeze[:, : cells.shape[0]], cells).astype(BF16)
            lsend[a, 48 * n : 48 * n + 48, :] = small
    pl.semaphore_wait(barrier, 16)
    for copy in halo_in:
        copy.start()
    for copy in params[1:]:
        copy.wait()
    gather(0)
    gather(1)
    project(0, 2)

    def receive_columns():
        for copy in halo_in[:2]:
            copy.wait()
        gather(2)
        project(864, 1)

    def receive_rows():
        for copy in halo_in[2:]:
            copy.wait()
        for a in range(2):
            base = dot(late[...], halo[a])
            for strip in range(3):
                for g in range(3):
                    at = strip * WIN + g * 48
                    got = dot(order[144:192, :], rows_of(a, strip, g)) + base[at : at + 48]
                    (tw, cw)[a][1296 + at : 1344 + at, :] = got.astype(BF16)
        project(1296, 1)

    def first_gradients():
        hidt[...] = hid[...].T
        for n in range(3):
            early.put(256 * n, dot(hidt[...], dproj[:, 512 * n : 512 * n + 256]))
            if n:
                early.cores[n - 1].start()

    def return_halo():
        for a in range(2):
            lout[a] = dot(late_t[...], res[a][1296:1728, :]).astype(BF16)
        for copy in halo_out[2:]:
            copy.start()
        for a in range(2):
            for g, runs in enumerate(groups(2)):
                cells = windows_of(a, 2, g)
                whole = dot(place[...], jnp.concatenate(cells, 0)).astype(BF16)
                at = 0
                for lev, c, n in runs:
                    to = slice((c - 24) * 24, (c - 24 + n) * 24)
                    region[a, lev, to, :] = whole[at * 24 : (at + n) * 24]
                    at += n
        for copy in halo_out[:2]:
            copy.start()
    def after_rows():
        early.step1a()
        early.step1b()
        outputs(864, 2)
        return_halo()

    @pl.loop(0, 7)
    def _(part):
        pl.when(part == 2)(receive_columns)
        pl.when(part == 4)(receive_rows)
        pl.when(part == 5)(first_gradients)
        pl.when(part == 6)(after_rows)
        pick = lambda values: sum(jnp.where(part == n, v, 0) for n, v in enumerate(values) if v)
        lo = pick((0, 256, 0, 256, 0, 256, 256))
        first = pick((0, 0, 6, 6, 9, 9, 4))
        count = pick((6, 4, 3, 3, 3, 3, 2))
        key_side = (lax.broadcasted_iota(jnp.int32, (WIN, 1), 0) % 6) >= 3
        lane = lax.broadcasted_iota(jnp.int32, (1, 256), 1)
        query = jnp.where(lane < 128, lane, 128 + lane % 16)
        differ = key_side != ((query % 6) >= 3)
        apart = jnp.logical_and(first == 9, lat == lats - 1)
        bias[...] = jnp.where(jnp.logical_and(apart, differ), -1e30, 0.0)

        @pl.loop(first, first + count)
        def _(w):
            attend(w, lo, proj, datt, bias, hm, hmf, att, dproj, bufs)

    attt[...] = att[...].T
    for n in range(5):
        if n < 3:
            grad = dot(hidt[...], dproj[:, 512 * n + 256 : 512 * n + 512])
        else:
            grad = dot(attt[...], cw[:, 256 * n - 768 : 256 * n - 512])
        final.put(256 * n, grad)
        if n in (2, 4):
            final.cores[n // 2 - 1].start()
    final.step1a()
    early.step2()
    outputs(0, 1)
    final.step1b()
    outputs(432, 1)
    early.step3()
    final.step2()
    final.step3()
    grads = early.result()
    for n in range(3):
        dqkv[:, 512 * n : 512 * n + 256] = grads[:, 256 * n : 256 * n + 256]

    for copy in halo_out:
        copy.wait()

    def with_first(cells, first):
        cells = cells.reshape(-1, 24, D)
        first = first.reshape(-1, 8, D)
        cells = jnp.concatenate([cells[:, 0:8] + first, cells[:, 8:24]], 1)
        return cells.reshape(-1, D).astype(BF16)

    for a, settled in enumerate((out, dtok)):
        rows = dot(spread[:96, :48], latin[a, 192:240, :])
        for level in range(2):
            cells = lonin[a, level].astype(F32)
            settled[level, 0:144, :] = with_first(cells, rows[48 * level : 48 * level + 48])
        rows = dot(spread[...], latin[a, 0:192, :])
        for strip in range(3):
            for g, runs in enumerate(groups(strip)):
                cells = windows_of(a, strip, g)
                whole = dot(place[...], jnp.concatenate(cells, 0))
                at = 0
                for lev, c, n in runs:
                    keep = min(n, max(0, 30 - c))
                    if keep:
                        top = (lev * 30 + c) * 8
                        part = with_first(
                            whole[at * 24 : (at + keep) * 24], rows[top : top + 8 * keep]
                        )
                        settled[lev, 144 + c * 24 : 144 + (c + keep) * 24, :] = part
                    at += n

    grads = final.result()
    for n in range(3):
        dqkv[:, 512 * n + 256 : 512 * n + 512] = grads[:, 256 * n : 256 * n + 256]
    dwo[...] = grads[:, 768:1280]


def per_device(tokens, gain, qkv_weight, out_weight, cotangent):
    by_column = lambda a: a.transpose(0, 2, 1, 3).reshape(2, 864, D)
    vmem = pl.BlockSpec(memory_space=pltpu.VMEM)
    hbm = pl.BlockSpec(memory_space=pl.ANY)
    buf = lambda *dims: pltpu.VMEM(dims, BF16)
    buf32 = lambda *dims: pltpu.VMEM(dims, F32)
    order, place, squeeze, last, last_t, spread, heads, heads32 = tables()
    copies = 12 + 2 * (2 + 6 + 6 + 3)

    def scatter(w):
        return [
            buf32(8, 32, 2 * w),
            buf(8, 32, 2 * w),
            buf(8, 32, 2 * w),
            buf(4, 2, 32, w),
            buf(3, 2, 32, w),
            buf(4, 4, 16, w),
            buf(3, 4, 16, w),
            buf(4, 16, w),
            buf(3, 16, w),
            buf(4, 16, w),
            buf(3, 16, w),
            buf32(2, 2, 8, w),
            buf32(3, 8, w),
            buf32(4, 4, 16, w),
            buf32(4, 16, w),
            buf32(4, 16, w),
        ]

    limit = 60 * 2**20
    out, dtok, dqkv, dwo = pl.pallas_call(
        kernel,
        out_shape=(
            pltpu.VMEM((2, 864, D), BF16),
            pltpu.VMEM((2, 864, D), BF16),
            pltpu.VMEM((4, 3 * D), F32),
            pltpu.VMEM((4, D), F32),
        ),
        in_specs=[hbm, hbm, vmem] + [hbm] * 10,
        out_specs=(vmem,) * 4,
        scratch_shapes=[
            buf(D, 3 * D),
            buf(D, D),
            *[buf(*t.shape) for t in (order, place, squeeze, last, last_t, spread, heads)],
            buf32(*heads32.shape),
            pltpu.SemaphoreType.DMA((10,)),
            buf(2, 2, 864, D),
            buf(2, 2, 144, D),
            buf(2, 240, D),
            buf(2, 240, D),
            buf(2, 2, 288, D),
            buf(2, 240, D),
            buf(2, 2, 144, D),
            buf(2, 240, D),
            buf(CELLS, D),
            buf(CELLS, D),
            buf(CELLS, D),
            buf(D, CELLS),
            buf(D, CELLS),
            buf32(CELLS, 1),
            buf32(CELLS, 1),
            buf(CELLS, 3 * D),
            buf(CELLS, D),
            buf(CELLS, D),
            buf(CELLS, 3 * D),
            buf32(WIN, 256),
            *[buf(WIN, 1152)] * 2,
            *[buf(128, 1152)] * 2,
            *[buf(1152, 256)] * 4,
            *scatter(384),
            *scatter(640),
            pltpu.SemaphoreType.DMA((4,)),
            pltpu.SemaphoreType.DMA((copies,)),
            pltpu.SemaphoreType.DMA((copies,)),
        ],
        compiler_params=pltpu.CompilerParams(
            collective_id=0, has_side_effects=True, vmem_limit_bytes=limit
        ),
        name="block",
    )(
        by_column(tokens),
        by_column(cotangent),
        gain.reshape(1, D),
        qkv_weight,
        out_weight,
        order,
        place,
        squeeze,
        last,
        last_t,
        spread,
        heads,
        heads32,
    )
    in_place = lambda a: a.reshape(2, 36, 24, D).transpose(0, 2, 1, 3)
    return in_place(out), in_place(dtok), dqkv, dwo


def solution(mesh):
    in_specs = (P(None, "lat", "lon", None), P(), P(), P(), P(None, "lat", "lon", None))
    out_specs = (
        P(None, "lat", "lon", None),
        P(None, "lat", "lon", None),
        P(("lon", "lat"), None),
        P(("lon", "lat"), None),
    )
    return jax.shard_map(
        per_device, mesh=mesh, in_specs=in_specs, out_specs=out_specs, check_vma=False
    )
```
